32 devices in a mesh: section: 4 (over y, x), batch: 8 (over z, core).
Axes of the slice: x: 2, y: 2, z: 4, core: 2. Of those that a mesh axis runs over, the one named last changes fastest.
Arguments:
- clean_mel: bfloat16 [16, 128, 80], P('batch'), may hold values from -6 to 6
- noise: bfloat16 [16, 128, 80], P('batch'), may hold values from -6 to 6
- phone_ids: int32 [16, 128], P('batch'), may hold values from 0 to 255
- segment_ids: int32 [16, 128], P('batch'), may hold values from 0 to 2, never falling along the last dimension, each value on 1 to 64 neighbouring positions
- loss_mask: int32 [16, 128], P('batch'), may hold values from 0 to 1, as said below
- time_idx: int32 [16], P('batch'), may hold values from 0 to 999
- attn_w: float32 [4, 2, 1024, 4096], P('section', None, 'batch')
- attn_m: float32 [4, 2, 1024, 4096], P('section', None, 'batch')
- attn_v: float32 [4, 2, 1024, 4096], P('section', None, 'batch'), as said below
- up_w: float32 [4, 2, 1024, 4096], P('section', None, 'batch'), may hold values from -0.1875 to 0.1875
- up_m: float32 [4, 2, 1024, 4096], P('section', None, 'batch')
- up_v: float32 [4, 2, 1024, 4096], P('section', None, 'batch'), as said below
- down_w: float32 [4, 2, 4096, 1024], P('section', None, 'batch'), may hold values from -0.09375 to 0.09375
- down_m: float32 [4, 2, 4096, 1024], P('section', None, 'batch')
- down_v: float32 [4, 2, 4096, 1024], P('section', None, 'batch'), as said below
- skip_w: float32 [4, 2048, 1024], P('section', 'batch'), may hold values from -0.125 to 0.125
- skip_m: float32 [4, 2048, 1024], P('section', 'batch')
- skip_v: float32 [4, 2048, 1024], P('section', 'batch'), as said below
- gain_w: float32 [4, 4, 1024], P('section', None, 'batch')
- gain_m: float32 [4, 4, 1024], P('section', None, 'batch')
- gain_v: float32 [4, 4, 1024], P('section', None, 'batch'), as said below
- table_w: float32 [497, 1024], replicated
- table_m: float32 [497, 1024], replicated
- table_v: float32 [497, 1024], replicated, as said below
Outputs:
- loss_sum: float32 [], replicated
- mask_total: float32 [], replicated
- grad_norm: float32 [], replicated
- attn_new: float32 [4, 2, 1024, 4096], P('section', None, 'batch')
- attn_first: float32 [4, 2, 1024, 4096], P('section', None, 'batch')
- attn_second: float32 [4, 2, 1024, 4096], P('section', None, 'batch')
- attn_copy: bfloat16 [4, 2, 1024, 4096], P('section', None, 'batch')
- up_new: float32 [4, 2, 1024, 4096], P('section', None, 'batch')
- up_first: float32 [4, 2, 1024, 4096], P('section', None, 'batch')
- up_second: float32 [4, 2, 1024, 4096], P('section', None, 'batch')
- up_copy: bfloat16 [4, 2, 1024, 4096], P('section', None, 'batch')
- down_new: float32 [4, 2, 4096, 1024], P('section', None, 'batch')
- down_first: float32 [4, 2, 4096, 1024], P('section', None, 'batch')
- down_second: float32 [4, 2, 4096, 1024], P('section', None, 'batch')
- down_copy: bfloat16 [4, 2, 4096, 1024], P('section', None, 'batch')
- skip_new: float32 [4, 2048, 1024], P('section', 'batch')
- skip_first: float32 [4, 2048, 1024], P('section', 'batch')
- skip_second: float32 [4, 2048, 1024], P('section', 'batch')
- skip_copy: bfloat16 [4, 2048, 1024], P('section', 'batch')
- gain_new: float32 [4, 4, 1024], P('section', None, 'batch')
- gain_first: float32 [4, 4, 1024], P('section', None, 'batch')
- gain_second: float32 [4, 4, 1024], P('section', None, 'batch')
- gain_copy: bfloat16 [4, 4, 1024], P('section', None, 'batch')
- table_new: float32 [497, 1024], replicated
- table_first: float32 [497, 1024], replicated
- table_second: float32 [497, 1024], replicated
- table_copy: bfloat16 [497, 1024], replicated
The draws below stay inside these ranges and needn't reach their ends.
Inputs may be any that keep to these rules, and one draw needn't show every extreme that they name: `loss_mask`: in the first row a frame counts with probability one quarter, rising evenly to three quarters in the last row; the first frame of every row counts. `attn_v`: positive. `up_v`: positive. `down_v`: positive. `skip_v`: positive. `gain_v`: positive. `table_v`: positive.
All inputs are finite; a program needn't handle non-finite values.
Results may differ from the reference program's by a relative error of at most 0.012.
The reference program's roundings to bfloat16 on the way count: a program that leaves them out, or rounds other values in their place, can miss the bound.
Values may be sent and summed in bfloat16 or wider, within the bound.
No kernel may reach another device: no remote copies, remote signals or barrier semaphores. Data moves between devices by JAX's collectives and lax.ppermute only.
A program may use at most 576 MiB of HBM per device.

```python
import math
import jax
import jax.numpy as jnp
import numpy as np
from jax import lax

D = 1024
HEADS = 16
FF = 4096
MEL = 80
VOCAB = 256
ROW = 128
TSTEPS = 1000
STEP = 10
PAIRS = 4
ROWS = 16
TABLE_ROWS = 497


clip_norm = 0.005


def grad_scale():
    return clip_norm / math.sqrt(PAIRS * (10 * D * D + 4 * D * FF + 4 * D) + TABLE_ROWS * D)


def first_moment(key, shape, spread):
    return jax.random.normal(key, shape, jnp.float32) * (0.111 * spread)


def second_moment(key, shape, spread):
    exponent = jax.random.uniform(key, shape, jnp.float32, math.log(0.001), math.log(0.004))
    return jnp.exp(exponent) * (spread * spread)


def rising_gain(key, shape):
    rising = 0.5 + jnp.arange(D, dtype=jnp.float32) / D
    return rising * jax.random.uniform(key, shape, jnp.float32, 0.8, 1.2)


def draw_loss_mask(key, part):
    key = jax.random.fold_in(key, 1)
    row_ids = jnp.arange(ROWS, dtype=jnp.int32)
    chance = 250 + 500 * row_ids // max(ROWS - 1, 1)
    dice_roll = jax.random.randint(key, (ROWS, ROW), 0, 1000)
    frame_mask = (dice_roll < chance[:, None]).astype(jnp.int32)
    return frame_mask.at[:, 0].set(1)


def draw_attn_w(key, part):
    key = jax.random.fold_in(key, 2)
    normal_part = jax.random.normal(key, (PAIRS, 2, D, 4 * D), jnp.float32) / math.sqrt(D)
    column_boost = jnp.where(jnp.arange(4 * D) >= 3 * D, 3.0, 1.0)
    return normal_part * column_boost


def draw_gain_w(key, part):
    key = jax.random.fold_in(key, 3)
    return rising_gain(key, (PAIRS, 4, D))


def draw_table_w(key, part):
    key = jax.random.fold_in(key, 4)
    normal_part = jax.random.normal(jax.random.fold_in(key, 1), (TABLE_ROWS, D), jnp.float32)
    row_index = jnp.arange(TABLE_ROWS)
    spread = jnp.where(row_index < 2 * MEL, 1.0 / math.sqrt(2 * MEL), jnp.where(row_index < 2 * MEL + VOCAB, 0.3, 1.0 / math.sqrt(D)))
    table_rows = normal_part * spread[:, None]
    return table_rows.at[TABLE_ROWS - 1].set(rising_gain(jax.random.fold_in(key, 2), (D,)))


def draw_attn_m(key, part):
    key = jax.random.fold_in(key, 11)
    return first_moment(key, (PAIRS, 2, D, 4 * D), grad_scale())


def draw_attn_v(key, part):
    key = jax.random.fold_in(key, 12)
    return second_moment(key, (PAIRS, 2, D, 4 * D), grad_scale())


def draw_up_m(key, part):
    key = jax.random.fold_in(key, 13)
    return first_moment(key, (PAIRS, 2, D, FF), grad_scale())


def draw_up_v(key, part):
    key = jax.random.fold_in(key, 14)
    return second_moment(key, (PAIRS, 2, D, FF), grad_scale())


def draw_down_m(key, part):
    key = jax.random.fold_in(key, 15)
    return first_moment(key, (PAIRS, 2, FF, D), grad_scale())


def draw_down_v(key, part):
    key = jax.random.fold_in(key, 16)
    return second_moment(key, (PAIRS, 2, FF, D), grad_scale())


def draw_skip_m(key, part):
    key = jax.random.fold_in(key, 17)
    return first_moment(key, (PAIRS, 2 * D, D), grad_scale())


def draw_skip_v(key, part):
    key = jax.random.fold_in(key, 18)
    return second_moment(key, (PAIRS, 2 * D, D), grad_scale())


def draw_gain_m(key, part):
    key = jax.random.fold_in(key, 19)
    return first_moment(key, (PAIRS, 4, D), 5.0 * grad_scale())


def draw_gain_v(key, part):
    key = jax.random.fold_in(key, 20)
    return second_moment(key, (PAIRS, 4, D), 5.0 * grad_scale())


def draw_table_m(key, part):
    key = jax.random.fold_in(key, 21)
    return first_moment(key, (TABLE_ROWS, D), grad_scale())


def draw_table_v(key, part):
    key = jax.random.fold_in(key, 22)
    return second_moment(key, (TABLE_ROWS, D), grad_scale())


def touch_ends(result, key, smallest, largest):
    longest = result.shape.index(max(result.shape))
    spots = []
    for shift in (0, 1):
        where = [jax.random.randint(jax.random.fold_in(key, axis), (), 0, length) for axis, length in enumerate(result.shape)]
        where[longest] = (where[longest] + shift) % result.shape[longest]
        spots.append(tuple(where))
    return result.at[spots[0]].set(smallest).at[spots[1]].set(largest)


def levels(rng, dims, pieces, smallest, top_value):
    level, own = 1.0, jax.random.fold_in(rng, 6)
    for dim, shards_of in pieces:
        steps = jnp.exp(jax.random.uniform(jax.random.fold_in(own, dim), (shards_of,), jnp.float32, smallest / len(pieces), top_value / len(pieces)))
        level = level * jnp.repeat(steps, dims[dim] // shards_of).reshape([-1 if axis == dim else 1 for axis in range(len(dims))])
    return level


def cumulative_ranks(number_of, skew):
    loads = [(1 << 20) // math.isqrt(standing ** skew) + 1 for standing in range(1, number_of + 1)]
    scale = 1 + sum(loads) // (1 << 30)
    return np.cumsum(np.array([max(1, weight // scale) for weight in loads]))


def ranked(own_key, dims, count, lean):
    listing = cumulative_ranks(count, lean)
    lot = jax.random.randint(jax.random.fold_in(own_key, 1), dims, 0, int(listing[count - 1]))
    grade = jnp.searchsorted(jnp.asarray(listing, jnp.int32), lot, side="right")
    return jax.random.permutation(jax.random.fold_in(own_key, 2), count)[grade].astype(jnp.int32)


def split_up(number_of, total, limit, skew):
    loads = [(1 << 20) // math.isqrt(rank ** skew) + 1 for rank in range(2, number_of + 1)]
    rest, counts = total - limit - (number_of - 1), [1] * (number_of - 1)
    while rest > 0:
        candidates = [i for i in range(number_of - 1) if counts[i] < limit]
        whole, remaining = sum([loads[i] for i in candidates]), rest
        for i in candidates:
            addition = min(limit - counts[i], max(1, remaining * loads[i] // whole), rest)
            counts[i] = counts[i] + addition
            rest = rest - addition
    return np.array([limit] + counts)


def ragged_sizes(stream_key, amount, total, limit, lean):
    if amount == 2:
        one = jax.random.randint(stream_key, (), max(1, total - limit), min(limit, total - 1) + 1)
        return jnp.stack([one, total - one])
    sizes = jnp.asarray(split_up(amount, total, limit, lean), jnp.int32)
    pairs = (amount - 1) // 2
    donor, sink = sizes[1:1 + 2 * pairs:2], sizes[2:2 + 2 * pairs:2]
    margin = jnp.minimum(donor - 1, limit - sink)
    passed = jax.random.randint(jax.random.fold_in(stream_key, 1), (pairs,), 0, 1 << 20) % (margin + 1)
    sizes = sizes.at[1:1 + 2 * pairs:2].set(donor - passed).at[2:2 + 2 * pairs:2].set(sink + passed)
    return sizes[jax.random.permutation(jax.random.fold_in(stream_key, 2), amount)]


def normal_values(key, shape, deviation, most, shards=(), held_as=jnp.bfloat16):
    entries = deviation * jax.random.normal(key, shape, jnp.float32)
    if shards:
        entries = entries * levels(key, shape, shards, -0.22, 0.18)
    return jnp.clip(entries, -most, most).astype(held_as)


def setup_inputs(seed: int = 0) -> dict:
    seeds = jax.random.split(jax.random.key(seed), 25)
    return {
        "clean_mel": normal_values(seeds[0], (ROWS, ROW, MEL), 1.0, 6.0, ((0, 8),)),
        "noise": normal_values(seeds[1], (ROWS, ROW, MEL), 1.0, 6.0, ((0, 8),)),
        "phone_ids": touch_ends(ranked(seeds[2], (ROWS, ROW), VOCAB, 2), jax.random.fold_in(seeds[2], 3), 0, VOCAB - 1).astype(jnp.int32),
        "segment_ids": jax.vmap(lambda own: jnp.searchsorted(jnp.cumsum(ragged_sizes(own, 3, ROW, ROW // 2, 2)), jnp.arange(ROW), side="right"))(jax.random.split(seeds[3], ROWS)).reshape((ROWS, ROW)).astype(jnp.int32),
        "loss_mask": draw_loss_mask(jax.random.fold_in(seeds[24], 71), 0),
        "time_idx": touch_ends(jax.random.randint(seeds[5], (ROWS,), 0, TSTEPS), jax.random.fold_in(seeds[5], 1), 0, TSTEPS - 1).astype(jnp.int32),
        "attn_w": draw_attn_w(jax.random.fold_in(seeds[24], 71), 0),
        "attn_m": draw_attn_m(jax.random.fold_in(seeds[24], 71), 0),
        "attn_v": draw_attn_v(jax.random.fold_in(seeds[24], 71), 0),
        "up_w": normal_values(seeds[9], (PAIRS, 2, D, FF), D ** -0.5, 0.1875, ((0, 4), (2, 8)), jnp.float32),
        "up_m": draw_up_m(jax.random.fold_in(seeds[24], 71), 0),
        "up_v": draw_up_v(jax.random.fold_in(seeds[24], 71), 0),
        "down_w": normal_values(seeds[12], (PAIRS, 2, FF, D), FF ** -0.5, 0.09375, ((0, 4), (2, 8)), jnp.float32),
        "down_m": draw_down_m(jax.random.fold_in(seeds[24], 71), 0),
        "down_v": draw_down_v(jax.random.fold_in(seeds[24], 71), 0),
        "skip_w": normal_values(seeds[15], (PAIRS, 2 * D, D), (2 * D) ** -0.5, 0.125, ((0, 4), (1, 8)), jnp.float32),
        "skip_m": draw_skip_m(jax.random.fold_in(seeds[24], 71), 0),
        "skip_v": draw_skip_v(jax.random.fold_in(seeds[24], 71), 0),
        "gain_w": draw_gain_w(jax.random.fold_in(seeds[24], 71), 0),
        "gain_m": draw_gain_m(jax.random.fold_in(seeds[24], 71), 0),
        "gain_v": draw_gain_v(jax.random.fold_in(seeds[24], 71), 0),
        "table_w": draw_table_w(jax.random.fold_in(seeds[24], 71), 0),
        "table_m": draw_table_m(jax.random.fold_in(seeds[24], 71), 0),
        "table_v": draw_table_v(jax.random.fold_in(seeds[24], 71), 0),
    }


@jax.custom_vjp
def low(v):
    return lax.optimization_barrier(v.astype(jnp.bfloat16)).astype(jnp.float32)

@jax.custom_vjp
def low_back(v):
    return v

def low_keep(v):
    return (low(v), None)

def low_pass(kept, grad):
    return (grad,)

def back_keep(v):
    return (v, None)

def back_low(kept, grad):
    return (low(grad),)
low.defvjp(low_keep, low_pass)
low_back.defvjp(back_keep, back_low)
norm_eps = 1e-05
beta_one = 0.9
beta_two = 0.999
adam_eps = 1e-08
rate_matrix = 0.02
rate_gain = 0.5
rate_table = 0.25
weight_decay = 0.01
clip_norm = 0.005
sigma_min = 1e-05

def dense_dot(left, right):
    return jnp.dot(left, right, precision=lax.Precision.HIGHEST)

def normalize(operand, gain):
    centered = operand - lax.optimization_barrier(jnp.mean(operand, axis=-1, keepdims=True))
    return centered * lax.rsqrt(lax.optimization_barrier(jnp.mean(centered * centered, axis=-1, keepdims=True)) + norm_eps) * gain

def alibi_bias(row_len):
    position = jnp.arange(row_len, dtype=jnp.float32)
    slopes = 2.0 ** (-8.0 * jnp.arange(1, HEADS + 1, dtype=jnp.float32) / HEADS)
    return -slopes[:, None, None] * jnp.abs(position[:, None] - position[None, :])[None]

def attend(qkv, segments):
    row_len = qkv.shape[0]
    model_dim = qkv.shape[1] // 3
    head_size = model_dim // HEADS
    split_qkv = qkv.reshape(row_len, 3, HEADS, head_size)
    scores = jnp.einsum('qhd,khd->hqk', split_qkv[:, 0], split_qkv[:, 1], precision=lax.Precision.HIGHEST) * head_size ** (-0.5)
    scores = scores + alibi_bias(row_len)
    allowed = segments[:, None] == segments[None, :]
    scores = jnp.where(allowed[None], scores, -1e+30)
    attn_probs = low(jax.nn.softmax(low_back(scores), axis=-1))
    context = jnp.einsum('hqk,khd->qhd', attn_probs, split_qkv[:, 2], precision=lax.Precision.HIGHEST)
    return context.reshape(row_len, model_dim)

def layer_apply(inputs, skip_in, w_attn, w_up, w_down, w_skip, gains, segments):
    model_dim = inputs.shape[1]
    if skip_in is None:
        residual = inputs
    else:
        residual = low_back(dense_dot(jnp.concatenate([inputs, skip_in], axis=1), w_skip))
    attn_in = low(normalize(residual, gains[0]))
    qkv = low(low_back(dense_dot(attn_in, w_attn[:, :3 * model_dim])))
    context = low(low_back(attend(qkv, segments)))
    middle = residual + low_back(dense_dot(context, w_attn[:, 3 * model_dim:]))
    ffn_in = low(normalize(middle, gains[1]))
    hidden = low_back(dense_dot(ffn_in, w_up))
    active = low(jax.nn.gelu(hidden, approximate=False))
    return middle + low_back(dense_dot(active, w_down))

def row_loss(weights, row_item):
    attn_all, up_all, down_all, skip_all, gains, front_table = weights
    clean_rows, noise_rows, phones, segments, frame_mask, step_index = row_item
    clean_rows = clean_rows.astype(jnp.float32)
    noise_rows = noise_rows.astype(jnp.float32)
    weight = frame_mask.astype(jnp.float32)
    flow_time = step_index.astype(jnp.float32) / TSTEPS
    noisy_mel = (1.0 - (1.0 - sigma_min) * flow_time) * noise_rows + flow_time * clean_rows
    context = clean_rows * (1.0 - weight)[:, None]
    target = clean_rows - (1.0 - sigma_min) * noise_rows
    mels = low(jnp.concatenate([noisy_mel, context], axis=1))
    onehot = (phones[:, None] == jnp.arange(VOCAB)[None, :]).astype(jnp.float32)
    half_dim = D // 2
    frequency = jnp.exp(-math.log(10000.0) * jnp.arange(half_dim, dtype=jnp.float32) / half_dim) * (1000.0 * flow_time)
    timing = jnp.concatenate([jnp.sin(frequency), jnp.cos(frequency)])
    state = low(dense_dot(mels, front_table[:2 * MEL]) + dense_dot(onehot, front_table[2 * MEL:2 * MEL + VOCAB]) + timing[None])
    skips = []
    for pair_idx in range(PAIRS):
        state = low(layer_apply(low_back(state), None, attn_all[pair_idx, 0], up_all[pair_idx, 0], down_all[pair_idx, 0], None, gains[pair_idx, 0:2], segments))
        skips.append(state)
    for pair_idx in reversed(range(PAIRS)):
        state = low(layer_apply(low_back(state), skips[pair_idx], attn_all[pair_idx, 1], up_all[pair_idx, 1], down_all[pair_idx, 1], skip_all[pair_idx], gains[pair_idx, 2:4], segments))
    normed = low(normalize(state, front_table[3 * MEL + VOCAB]))
    predicted = low_back(dense_dot(normed, front_table[2 * MEL + VOCAB:3 * MEL + VOCAB].T))
    error_mel = predicted - target
    return jnp.sum(weight * lax.optimization_barrier(jnp.mean(error_mel * error_mel, axis=-1)))

def adam_update(master, first, second, gradient, factor, step_rate):
    gradient = gradient * factor
    first_new = beta_one * first + (1.0 - beta_one) * gradient
    second_new = beta_two * second + (1.0 - beta_two) * gradient * gradient
    corrected = first_new / (1.0 - beta_one ** STEP)
    spread = jnp.sqrt(second_new / (1.0 - beta_two ** STEP))
    master_new = master - step_rate * (corrected / (spread + adam_eps) + weight_decay * master)
    return (master_new, first_new, second_new, master_new.astype(jnp.bfloat16))

def reference(clean_mel, noise, phone_ids, segment_ids, loss_mask, time_idx, attn_w, attn_m, attn_v, up_w, up_m, up_v, down_w, down_m, down_v, skip_w, skip_m, skip_v, gain_w, gain_m, gain_v, table_w, table_m, table_v):
    masters = (attn_w, up_w, down_w, skip_w, gain_w, table_w)
    rounded = tuple((master.astype(jnp.bfloat16).astype(jnp.float32) for master in masters))
    mask_total = jnp.sum(loss_mask.astype(jnp.float32))
    row_data = (clean_mel, noise, phone_ids, segment_ids, loss_mask, time_idx)

    def objective(weights):

        def accumulate(running, row_item):
            return (running + jax.checkpoint(row_loss)(weights, row_item), None)
        loss_sum, _ = lax.scan(accumulate, jnp.zeros((), jnp.float32), row_data)
        return (loss_sum / mask_total, loss_sum)
    _, backward, loss_sum = jax.vjp(objective, rounded, has_aux=True)
    gradients = backward(jnp.ones((), jnp.float32))[0]
    grad_norm = jnp.sqrt(sum((jnp.sum(grad_arr * grad_arr) for grad_arr in gradients)))
    factor = clip_norm / jnp.maximum(grad_norm, clip_norm)
    attn_out = adam_update(attn_w, attn_m, attn_v, gradients[0], factor, rate_matrix)
    up_out = adam_update(up_w, up_m, up_v, gradients[1], factor, rate_matrix)
    down_out = adam_update(down_w, down_m, down_v, gradients[2], factor, rate_matrix)
    skip_out = adam_update(skip_w, skip_m, skip_v, gradients[3], factor, rate_matrix)
    gain_out = adam_update(gain_w, gain_m, gain_v, gradients[4], factor, rate_gain)
    table_out = adam_update(table_w, table_m, table_v, gradients[5], factor, rate_table)
    return (loss_sum, mask_total, grad_norm, attn_out[0], attn_out[1], attn_out[2], attn_out[3], up_out[0], up_out[1], up_out[2], up_out[3], down_out[0], down_out[1], down_out[2], down_out[3], skip_out[0], skip_out[1], skip_out[2], skip_out[3], gain_out[0], gain_out[1], gain_out[2], gain_out[3], table_out[0], table_out[1], table_out[2], table_out[3])
```

```python
import math

import jax
import jax.numpy as jnp
from jax import lax
from jax.experimental import pallas as pl
from jax.experimental.pallas import tpu as pltpu
from jax.sharding import PartitionSpec as P

HEADS = 16
VOCAB = 256
TSTEPS = 1000
STEP = 10

norm_eps = 1e-05
beta_one = 0.9
beta_two = 0.999
adam_eps = 1e-08
rate_matrix = 0.02
rate_gain = 0.5
rate_table = 0.25
weight_decay = 0.01
clip_norm = 0.005
sigma_min = 1e-05

LAG = 2
BOTH = ("section", "batch")
BF16 = jnp.bfloat16
F32 = jnp.float32
BLOCK = 1024
SLOPES = [2.0 ** (-8.0 * (head + 1) / HEADS) for head in range(HEADS)]
VMEM_LIMIT = 16 * 2**20
QUICK = pl.CostEstimate(flops=1, bytes_accessed=1, transcendentals=0)


def to_low(operand):
    return operand.astype(BF16)


def matmul(left, right):
    return jnp.dot(left, right, preferred_element_type=F32)


def matmul_nt(left, right):
    return lax.dot_general(left, right, (((1,), (1,)), ((), ())), preferred_element_type=F32)


def matmul_tn(left, right):
    return lax.dot_general(left, right, (((0,), (0,)), ((), ())), preferred_element_type=F32)


def normalize(operand, gain):
    centered = operand - jnp.mean(operand, axis=-1, keepdims=True)
    variance = jnp.mean(centered * centered, axis=-1, keepdims=True)
    return centered * lax.rsqrt(variance + norm_eps) * gain


def normalize_back(grad, operand, gain):
    centered = operand - jnp.mean(operand, axis=-1, keepdims=True)
    scale = lax.rsqrt(jnp.mean(centered * centered, axis=-1, keepdims=True) + norm_eps)
    unit = centered * scale
    scaled = grad * gain
    along = jnp.mean(scaled * unit, axis=-1, keepdims=True)
    back = scale * (scaled - jnp.mean(scaled, axis=-1, keepdims=True) - unit * along)
    return back, jnp.sum(grad * unit, axis=0, keepdims=True)


def head_masks(rows):
    lanes = lax.broadcasted_iota(jnp.int32, (rows, 128), 1)
    return lanes < 64


def split_heads(slab, low_half):
    zero = jnp.zeros_like(slab)
    return jnp.concatenate(
        [jnp.where(low_half, slab, zero), jnp.where(low_half, zero, slab)], axis=0
    )


def live_slot(base, tick, steps_before):
    lag_count = tick - steps_before
    return (lag_count >= 0) & (lag_count < base[4]), jnp.clip(lag_count, 0, base[5] - 1)


def forward_kernel(
    base, tick_ref, arrived, embedded, skip_a, skip_b, skip_c, allowed, in_flight, gains,
    w_skip, w_attn, w_up, w_down,
    in_join, in_res, in_ain, in_qkv, in_prob, in_ctx, in_mid, in_fin, in_act, in_slope, in_final,
    leaving, o_join, o_res, o_ain, o_qkv, o_prob, o_ctx, o_mid, o_fin, o_act, o_slope, o_final,
    same_skip, same_attn, same_up, same_down,
    join, allow, res, ain, qkv, prob, ctx, mid, fin, act, slope, sent, acc, sem_in, sem_out,
):
    is_dec, pair, pos = base[0], base[1], base[2]
    is_live, slot = live_slot(base, tick_ref[0], LAG * pos + base[3])
    rows, width = res.shape
    hidden_size = act.shape[1]

    @pl.when(is_live)
    def _():
        first_half = join.at[:, pl.ds(0, width)]
        second_half = join.at[:, pl.ds(width, width)]
        from_rows = pltpu.make_async_copy(embedded.at[slot], first_half, sem_in.at[0])
        from_chain = pltpu.make_async_copy(arrived, first_half, sem_in.at[0])
        mask_copy = pltpu.make_async_copy(allowed.at[slot], allow, sem_in.at[2])
        skips = [
            pltpu.make_async_copy(source, second_half, sem_in.at[1])
            for source in (skip_a, skip_b, skip_c, arrived)
        ]

        @pl.when(pos == 0)
        def _():
            from_rows.start()

        @pl.when(pos != 0)
        def _():
            from_chain.start()

        @pl.when(is_dec == 1)
        def _():
            for which in range(4):

                @pl.when(pair == which)
                def _():
                    skips[which].start()

        mask_copy.start()
        from_chain.wait()
        outgoing = []

        def keep(source, target, index):
            copy = pltpu.make_async_copy(source, target.at[slot], sem_out.at[index])
            copy.start()
            outgoing.append(copy)

        @pl.when(is_dec == 1)
        def _():
            skips[0].wait()
            for start in range(0, width, BLOCK):
                cut = slice(start, start + BLOCK)
                res[:, cut] = matmul(join[...], w_skip[:, cut])

        @pl.when(is_dec == 0)
        def _():
            res[...] = join[:, :width].astype(F32)

        keep(join, o_join, 0)
        keep(res, o_res, 1)
        ain[...] = to_low(normalize(res[...], gains[0:1, :]))
        keep(ain, o_ain, 2)
        for start in range(0, 3 * width, BLOCK):
            cut = slice(start, start + BLOCK)
            qkv[:, cut] = to_low(matmul(ain[...], w_attn[:, cut]))
        keep(qkv, o_qkv, 3)
        mask_copy.wait()
        row_ids = lax.broadcasted_iota(jnp.int32, (rows, rows), 0)
        col_ids = lax.broadcasted_iota(jnp.int32, (rows, rows), 1)
        distance = jnp.abs(row_ids - col_ids).astype(F32)
        is_allowed = allow[...] > 0.5
        low_half = head_masks(rows)
        for two in range(HEADS // 2):
            cut = slice(two * 128, two * 128 + 128)
            queries = split_heads(qkv[:, cut], low_half)
            keys = qkv[:, width + two * 128 : width + two * 128 + 128]
            scores = matmul_nt(queries, keys) * 0.125
            prob[2 * two] = scores[:rows]
            prob[2 * two + 1] = scores[rows:]
        for head in range(HEADS):
            scores = jnp.where(is_allowed, prob[head] + (-SLOPES[head]) * distance, -1e30)
            powers = jnp.exp(scores - jnp.max(scores, axis=-1, keepdims=True))
            prob[head] = powers * (1.0 / jnp.sum(powers, axis=-1, keepdims=True))
        for two in range(HEADS // 2):
            cut = slice(two * 128, two * 128 + 128)
            values = qkv[:, 2 * width + two * 128 : 2 * width + two * 128 + 128]
            chances = jnp.concatenate([to_low(prob[2 * two]), to_low(prob[2 * two + 1])], axis=0)
            mixed = matmul(chances, values)
            ctx[:, cut] = to_low(jnp.where(low_half, mixed[:rows], mixed[rows:]))
        keep(prob, o_prob, 4)
        keep(ctx, o_ctx, 5)
        for start in range(0, width, BLOCK):
            cut = slice(start, start + BLOCK)
            column = 3 * width + start
            mid[:, cut] = res[:, cut] + matmul(ctx[...], w_attn[:, column : column + BLOCK])
        keep(mid, o_mid, 6)
        fin[...] = to_low(normalize(mid[...], gains[1:2, :]))
        keep(fin, o_fin, 7)
        for start in range(0, hidden_size, BLOCK):
            cut = slice(start, start + BLOCK)
            hidden = matmul(fin[...], w_up[:, cut])
            below = 0.5 + 0.5 * lax.erf(hidden * (2.0**-0.5))
            density = (2.0 * math.pi) ** -0.5 * jnp.exp(-0.5 * hidden * hidden)
            act[:, cut] = to_low(hidden * below)
            slope[:, cut] = to_low(below + hidden * density)
            part = matmul(act[:, cut], w_down[cut, :])
            if start == 0:
                acc[...] = part
            else:
                acc[...] += part
        keep(act, o_act, 8)
        keep(slope, o_slope, 9)
        sent[...] = to_low(mid[...] + acc[...])

        @pl.when(pos == base[6])
        def _():
            last = pltpu.make_async_copy(sent, o_final.at[slot], sem_in.at[1])
            last.start()
            last.wait()

        leave = pltpu.make_async_copy(sent, leaving, sem_in.at[0])
        leave.start()
        leave.wait()
        for copy in outgoing:
            copy.wait()


def backward_kernel(
    base, tick_ref, arrived, head_grads, skip_a, skip_b, skip_c, in_flight, gains,
    w_skip, w_attn, w_up, w_down, k_res, k_qkv, k_prob, k_mid, k_slope,
    in_branch, in_hid, in_proj, in_qkvg, in_resg, in_gain,
    leaving, leaving_skip, o_branch, o_hid, o_proj, o_qkvg, o_resg, o_gain,
    same_skip, same_attn, same_up, same_down,
    x_low, x_wide, x_skip, res, qkv, prob, mid, slope, grad, branch, hid, proj, qkvg, resg, gain_g,
    acc, ctx_g, joined, sem_in, sem_out,
):
    is_dec, pair, pos = base[0], base[1], base[2]
    is_live, slot = live_slot(base, tick_ref[0], LAG * (base[6] - pos))
    is_last = pos == base[6]
    rows, width = res.shape
    hidden_size = hid.shape[1]

    @pl.when(is_live)
    def _():
        from_head = pltpu.make_async_copy(head_grads.at[slot], x_wide, sem_in.at[0])
        from_chain = pltpu.make_async_copy(arrived, x_low, sem_in.at[1])
        skips = [
            pltpu.make_async_copy(source, x_skip, sem_in.at[2])
            for source in (skip_a, skip_b, skip_c)
        ]
        kept = [
            pltpu.make_async_copy(source.at[slot], target, sem_in.at[3 + index])
            for index, (source, target) in enumerate(
                ((k_slope, slope), (k_mid, mid), (k_prob, prob), (k_qkv, qkv), (k_res, res))
            )
        ]
        with_skip = (is_dec == 0) & (pair < 3)

        @pl.when(is_last)
        def _():
            from_head.start()

        @pl.when(jnp.logical_not(is_last))
        def _():
            from_chain.start()

        @pl.when(with_skip)
        def _():
            for which in range(3):

                @pl.when(pair == which)
                def _():
                    skips[which].start()

        for copy in kept:
            copy.start()
        outgoing = []

        def keep(source, target, index):
            copy = pltpu.make_async_copy(source, target.at[slot], sem_out.at[index])
            copy.start()
            outgoing.append(copy)

        @pl.when(is_last)
        def _():
            from_head.wait()
            grad[...] = x_wide[...]

        @pl.when(jnp.logical_not(is_last))
        def _():
            from_chain.wait()
            grad[...] = x_low[...].astype(F32)

        @pl.when(with_skip)
        def _():
            skips[0].wait()
            grad[...] += x_skip[...].astype(F32)

        branch[...] = to_low(grad[...])
        keep(branch, o_branch, 0)
        kept[0].wait()
        for start in range(0, hidden_size, BLOCK):
            cut = slice(start, start + BLOCK)
            hidden_low = to_low(matmul(branch[...], w_down[:, cut]) * slope[:, cut].astype(F32))
            hid[:, cut] = hidden_low
            part = matmul(hidden_low, w_up[cut, :])
            if start == 0:
                acc[...] = part
            else:
                acc[...] += part
        keep(hid, o_hid, 1)
        kept[1].wait()
        back, gain_back = normalize_back(acc[...], mid[...], gains[1:2, :])
        gain_g[1:2, :] = gain_back
        grad[...] += back
        proj[...] = to_low(grad[...])
        keep(proj, o_proj, 2)
        for start in range(0, width, BLOCK):
            cut = slice(start, start + BLOCK)
            ctx_g[:, cut] = to_low(matmul(proj[...], w_attn[3 * width :, cut]))
        kept[2].wait()
        kept[3].wait()
        low_half = head_masks(rows)
        for two in range(HEADS // 2):
            cut = slice(two * 128, two * 128 + 128)
            key_cut = slice(width + two * 128, width + two * 128 + 128)
            value_cut = slice(2 * width + two * 128, 2 * width + two * 128 + 128)
            outer_grad = split_heads(ctx_g[:, cut], low_half)
            prob_grad = matmul_nt(outer_grad, qkv[:, value_cut])
            chances = jnp.concatenate([prob[2 * two], prob[2 * two + 1]], axis=0)
            qkvg[:, value_cut] = to_low(matmul_tn(to_low(chances), outer_grad))
            total = jnp.sum(prob_grad * chances, axis=-1, keepdims=True)
            score_grad = to_low(chances * (prob_grad - total))
            query_grad = matmul(score_grad, qkv[:, key_cut]) * 0.125
            qkvg[:, cut] = to_low(jnp.where(low_half, query_grad[:rows], query_grad[rows:]))
            queries = split_heads(qkv[:, cut], low_half)
            qkvg[:, key_cut] = to_low(matmul_tn(score_grad, queries) * 0.125)
        keep(qkvg, o_qkvg, 3)
        for start in range(0, 3 * width, BLOCK):
            cut = slice(start, start + BLOCK)
            part = matmul(qkvg[:, cut], w_attn[cut, :])
            if start == 0:
                acc[...] = part
            else:
                acc[...] += part
        kept[4].wait()
        back, gain_back = normalize_back(acc[...], res[...], gains[0:1, :])
        gain_g[0:1, :] = gain_back
        gain_g[2:8, :] = jnp.zeros((6, width), F32)
        keep(gain_g, o_gain, 5)
        grad[...] += back
        resg[...] = to_low(grad[...])
        keep(resg, o_resg, 4)

        @pl.when(is_dec == 1)
        def _():
            for start in range(0, width, BLOCK):
                cut = slice(start, start + BLOCK)
                skip_cut = slice(width + start, width + start + BLOCK)
                input_grad = to_low(matmul(resg[...], w_skip[:, cut]))
                skip_grad = matmul(resg[...], w_skip[:, skip_cut])
                both = to_low(input_grad.astype(F32) + skip_grad)
                joined[:, cut] = jnp.where(pair == 3, both, input_grad)
                joined[:, skip_cut] = to_low(skip_grad)
            first = pltpu.make_async_copy(joined.at[:, pl.ds(0, width)], leaving, sem_in.at[0])
            second = pltpu.make_async_copy(
                joined.at[:, pl.ds(width, width)], leaving_skip, sem_in.at[1]
            )
            first.start()
            second.start()
            first.wait()
            second.wait()

        @pl.when(is_dec == 0)
        def _():
            first = pltpu.make_async_copy(resg, leaving, sem_in.at[0])
            first.start()
            first.wait()

        for copy in outgoing:
            copy.wait()


def kept_shapes(slots, rows, width, hidden_size):
    return [
        ((slots, rows, 2 * width), BF16),
        ((slots, rows, width), F32),
        ((slots, rows, width), BF16),
        ((slots, rows, 3 * width), BF16),
        ((slots, HEADS, rows, rows), F32),
        ((slots, rows, width), BF16),
        ((slots, rows, width), F32),
        ((slots, rows, width), BF16),
        ((slots, rows, hidden_size), BF16),
        ((slots, rows, hidden_size), BF16),
        ((slots, rows, width), BF16),
    ]


def grad_shapes(slots, rows, width, hidden_size):
    return [
        ((slots, rows, width), BF16),
        ((slots, rows, hidden_size), BF16),
        ((slots, rows, width), BF16),
        ((slots, rows, 3 * width), BF16),
        ((slots, rows, width), BF16),
        ((slots, 8, width), F32),
    ]


ANYWHERE = pl.BlockSpec(memory_space=pl.ANY)
IN_HBM = pl.BlockSpec(memory_space=pltpu.HBM)
IN_VMEM = pl.BlockSpec(memory_space=pltpu.VMEM)
IN_SMEM = pl.BlockSpec(memory_space=pltpu.SMEM)


def stay_in_hbm(array):
    return pltpu.with_memory_space_constraint(array, pltpu.HBM)


def all_ordered(arrays, earlier):
    count = len(arrays)
    return list(
        pl.pallas_call(
            lambda *refs: None,
            out_shape=[pltpu.HBM(array.shape, array.dtype) for array in arrays],
            in_specs=[IN_HBM] * (count + 1),
            out_specs=[IN_HBM] * count,
            input_output_aliases={index: index for index in range(count)},
            compiler_params=pltpu.CompilerParams(vmem_limit_bytes=2**20),
            cost_estimate=QUICK,
            name="ordered",
        )(*arrays, earlier)
    )


def ordered(array, earlier):
    return all_ordered([array], earlier)[0]


def same_in_vmem(arrays):
    return [pltpu.VMEM(array.shape, array.dtype) for array in arrays]


def unwritten(shapes):
    return list(
        pl.pallas_call(
            lambda *refs: None,
            out_shape=[pltpu.HBM(shape, dtype) for shape, dtype in shapes],
            out_specs=[IN_HBM] * len(shapes),
            compiler_params=pltpu.CompilerParams(vmem_limit_bytes=2**20),
            cost_estimate=QUICK,
            name="unwritten",
        )()
    )


def one_slot(shapes):
    return [pltpu.VMEM(shape[1:], dtype) for shape, dtype in shapes]


def forward_tick(base, tick, arrived, embedded, skips, allowed, in_flight, gains, weights, kept):
    slots, rows, width = embedded.shape
    hidden_size = weights[2].shape[1]
    shapes = kept_shapes(slots, rows, width, hidden_size)
    outputs = pl.pallas_call(
        forward_kernel,
        out_shape=[jax.ShapeDtypeStruct((rows, width), BF16)]
        + [pltpu.HBM(shape, dtype) for shape, dtype in shapes]
        + same_in_vmem(weights),
        in_specs=[IN_SMEM] * 2 + [ANYWHERE] * 7 + [IN_VMEM] * 5 + [IN_HBM] * 11,
        out_specs=[ANYWHERE] + [IN_HBM] * 11 + [IN_VMEM] * 4,
        input_output_aliases={14 + index: 1 + index for index in range(11)}
        | {10 + index: 12 + index for index in range(4)},
        scratch_shapes=one_slot(shapes[:1])
        + [pltpu.VMEM((rows, rows), F32)]
        + one_slot(shapes[1:])
        + [
            pltpu.VMEM((rows, width), F32),
            pltpu.SemaphoreType.DMA((3,)),
            pltpu.SemaphoreType.DMA((10,)),
        ],
        compiler_params=pltpu.CompilerParams(vmem_limit_bytes=VMEM_LIMIT),
        cost_estimate=QUICK,
        name="layer_forward",
    )(
        base,
        jnp.array([tick], jnp.int32),
        arrived,
        embedded,
        *skips,
        allowed,
        in_flight,
        gains,
        *weights,
        *kept,
    )
    return outputs[0], list(outputs[1:12]), list(outputs[12:])


def backward_tick(
    base, tick, arrived, head_grads, skips, in_flight, gains, weights, kept, grads
):
    slots, rows, width = head_grads.shape
    hidden_size = weights[2].shape[0]
    shapes = grad_shapes(slots, rows, width, hidden_size)
    was_kept = kept_shapes(slots, rows, width, hidden_size)
    read = [1, 3, 4, 6, 9]
    outputs = pl.pallas_call(
        backward_kernel,
        out_shape=[jax.ShapeDtypeStruct((rows, width), BF16)] * 2
        + [pltpu.HBM(shape, dtype) for shape, dtype in shapes]
        + same_in_vmem(weights),
        in_specs=[IN_SMEM] * 2 + [ANYWHERE] * 6 + [IN_VMEM] * 5 + [IN_HBM] * 11,
        out_specs=[ANYWHERE] * 2 + [IN_HBM] * 6 + [IN_VMEM] * 4,
        input_output_aliases={18 + index: 2 + index for index in range(6)}
        | {9 + index: 8 + index for index in range(4)},
        scratch_shapes=[
            pltpu.VMEM((rows, width), BF16),
            pltpu.VMEM((rows, width), F32),
            pltpu.VMEM((rows, width), BF16),
        ]
        + one_slot([was_kept[index] for index in read])
        + [pltpu.VMEM((rows, width), F32)]
        + one_slot(shapes)
        + [
            pltpu.VMEM((rows, width), F32),
            pltpu.VMEM((rows, width), BF16),
            pltpu.VMEM((rows, 2 * width), BF16),
            pltpu.SemaphoreType.DMA((8,)),
            pltpu.SemaphoreType.DMA((6,)),
        ],
        compiler_params=pltpu.CompilerParams(vmem_limit_bytes=VMEM_LIMIT),
        cost_estimate=QUICK,
        name="layer_backward",
    )(
        base,
        jnp.array([tick], jnp.int32),
        arrived,
        head_grads,
        *skips,
        in_flight,
        gains,
        *weights,
        *[stay_in_hbm(kept[index]) for index in read],
        *grads,
    )
    return outputs[0], outputs[1], list(outputs[2:8]), list(outputs[8:])


def transposed_shapes(weights):
    return [(weight.shape[::-1], BF16) for weight in weights]


def transpose_half(base, weight, target, half, for_dec):
    block = min(512, *weight.shape)

    def kernel(base_ref, source, start, same, out, stage, sems):
        @pl.when((base_ref[0] == (1 if for_dec else 0)) & (base_ref[7] == 0))
        def _():
            waiting = [None, None]
            steps = [
                (row, column)
                for row in range(0, source.shape[0], block)
                for column in range(0, source.shape[1], block)
            ]
            middle = len(steps) // 2
            steps = steps[middle:] if half else steps[:middle]
            for index, (row, column) in enumerate(steps):
                slot = index % 2
                if waiting[slot] is not None:
                    waiting[slot].wait()
                stage[slot] = source[row : row + block, column : column + block].T
                target = out.at[pl.ds(column, block), pl.ds(row, block)]
                waiting[slot] = pltpu.make_async_copy(stage.at[slot], target, sems.at[slot])
                waiting[slot].start()
            for copy in waiting:
                copy.wait()

    return pl.pallas_call(
        kernel,
        out_shape=[*same_in_vmem([weight]), pltpu.HBM(target.shape, target.dtype)],
        in_specs=[IN_SMEM, IN_VMEM, IN_HBM],
        out_specs=[IN_VMEM, IN_HBM],
        input_output_aliases={1: 0, 2: 1},
        scratch_shapes=[pltpu.VMEM((2, block, block), BF16), pltpu.SemaphoreType.DMA((2,))],
        compiler_params=pltpu.CompilerParams(vmem_limit_bytes=VMEM_LIMIT),
        cost_estimate=QUICK,
        name="transpose_half",
    )(base, weight, target)


def head_pass(
    base, final, target, frame_weight, head_rows, out_gain, scale, mel_bins, transposed
):
    slots, rows, width = final.shape
    count_weights = len(transposed)
    def kernel(
        base_ref, scale_ref, final_ref, target_ref, weight_ref, head_ref, gain_ref, *refs
    ):
        sources = refs[:count_weights]
        grads_ref, table_ref, gain_grad_ref, loss_ref = refs[count_weights : count_weights + 4]
        wholes = refs[count_weights + 4 : 2 * count_weights + 4]
        x_buf, out_buf, s_in, s_out, s_weights = refs[2 * count_weights + 4 :]
        moves = [
            pltpu.make_async_copy(source, whole, s_weights.at[index])
            for index, (source, whole) in enumerate(zip(sources, wholes))
        ]

        @pl.when(base_ref[7] == 0)
        def _():
            for move in moves:
                move.start()

        table_ref[...] = jnp.zeros((mel_bins, width), F32)
        gain_grad_ref[...] = jnp.zeros((1, width), F32)
        loss_ref[...] = jnp.zeros((rows, 128), F32)
        is_last = base_ref[2] == base_ref[6]
        count = base_ref[4]

        def row(i):
            load = pltpu.make_async_copy(final_ref.at[i], x_buf.at[i], s_in.at[i])
            load.wait()
            wide = x_buf[i].astype(F32)
            normed = to_low(normalize(wide, gain_ref[...]))
            error = matmul_nt(normed, head_ref[...]) - target_ref[i]
            weight = weight_ref[i]
            loss_ref[...] += weight * (error * error) * (1.0 / mel_bins)
            d_pred = to_low(error * weight * scale_ref[0])
            table_ref[...] += matmul_tn(d_pred, normed)[:mel_bins]
            back, gain_back = normalize_back(matmul(d_pred, head_ref[...]), wide, gain_ref[...])
            gain_grad_ref[...] += gain_back
            out_buf[i] = back
            pltpu.make_async_copy(out_buf.at[i], grads_ref.at[i], s_out.at[i]).start()

        @pl.when(is_last)
        def _():
            for i in range(slots):

                @pl.when(i < count)
                def _():
                    pltpu.make_async_copy(final_ref.at[i], x_buf.at[i], s_in.at[i]).start()

            for i in range(slots):
                pl.when(i < count)(lambda i=i: row(i))
            for i in range(slots):

                @pl.when(i < count)
                def _():
                    pltpu.make_async_copy(out_buf.at[i], grads_ref.at[i], s_out.at[i]).wait()

        @pl.when(base_ref[7] == 0)
        def _():
            for move in moves:
                move.wait()

    return pl.pallas_call(
        kernel,
        out_shape=[
            pltpu.HBM((slots, rows, width), F32),
            jax.ShapeDtypeStruct((mel_bins, width), F32),
            jax.ShapeDtypeStruct((1, width), F32),
            jax.ShapeDtypeStruct((rows, 128), F32),
        ]
        + same_in_vmem(transposed),
        in_specs=[IN_SMEM] * 2 + [IN_HBM] + [IN_VMEM] * 4 + [IN_HBM] * count_weights,
        out_specs=[IN_HBM] + [IN_VMEM] * (3 + count_weights),
        scratch_shapes=[
            pltpu.VMEM((slots, rows, width), BF16),
            pltpu.VMEM((slots, rows, width), F32),
            pltpu.SemaphoreType.DMA((slots,)),
            pltpu.SemaphoreType.DMA((slots,)),
            pltpu.SemaphoreType.DMA((count_weights,)),
        ],
        compiler_params=pltpu.CompilerParams(vmem_limit_bytes=VMEM_LIMIT),
        cost_estimate=QUICK,
        name="head_pass",
    )(base, scale, final, target, frame_weight, head_rows, out_gain, *transposed)


def table_pass(
    base, front, input_grads, gain_grads, head_total, out_gain_total, table_rows, earlier
):
    slots, rows, width = input_grads.shape
    front_rows, mel_bins = front.shape[1], head_total.shape[0]

    def kernel(
        base_ref, front_ref, grad_ref, gain_ref, earlier_ref, head_ref, out_ref, block_ref, x, y, g, sems
    ):
        is_dec = base_ref[0] == 1
        is_outer = base_ref[7] == 1
        block_ref[...] = jnp.zeros((table_rows + 16, width), BF16)
        tail = table_rows - front_rows - mel_bins
        block_ref[front_rows : front_rows + mel_bins, :] = to_low(head_ref[...])
        first = lax.broadcasted_iota(jnp.int32, (tail, width), 0) == 0
        block_ref[front_rows + mel_bins : table_rows, :] = to_low(
            jnp.where(first, out_ref[...], 0.0)
        )

        @pl.when(jnp.logical_not(is_outer))
        def _():
            load = pltpu.make_async_copy(gain_ref, g, sems.at[2])
            load.start()
            load.wait()
            total = g[0]
            for i in range(1, slots):
                total = total + g[i]
            own = jnp.concatenate([total, jnp.zeros((8, width), F32)], axis=0)
            moved = jnp.concatenate([jnp.zeros((2, width), F32), own[:14]], axis=0)
            block_ref[table_rows:, :] = to_low(jnp.where(is_dec, moved, own))

        @pl.when((base_ref[2] == 0) & jnp.logical_not(is_outer))
        def _():
            loads = [
                pltpu.make_async_copy(front_ref, x, sems.at[0]),
                pltpu.make_async_copy(grad_ref, y, sems.at[1]),
            ]
            for load in loads:
                load.start()
            for load in loads:
                load.wait()
            product = matmul_tn(x[...], y[...].reshape(slots * rows, width))
            block_ref[:front_rows, :] = to_low(product)

    return pl.pallas_call(
        kernel,
        out_shape=jax.ShapeDtypeStruct((table_rows + 16, width), BF16),
        in_specs=[IN_SMEM] + [IN_HBM] * 4 + [IN_VMEM] * 2,
        out_specs=IN_VMEM,
        scratch_shapes=[
            pltpu.VMEM(front.shape, BF16),
            pltpu.VMEM(input_grads.shape, BF16),
            pltpu.VMEM(gain_grads.shape, F32),
            pltpu.SemaphoreType.DMA((3,)),
        ],
        compiler_params=pltpu.CompilerParams(vmem_limit_bytes=VMEM_LIMIT),
        cost_estimate=QUICK,
        name="table_pass",
    )(
        base, stay_in_hbm(front), input_grads, gain_grads, stay_in_hbm(earlier), head_total,
        out_gain_total,
    )


def assemble(base, main_shards, skip_shards, span, width, hidden_size):
    main = [part for group in main_shards for part in group]
    skip = [part for group in skip_shards for part in group]
    sides = hidden_size // width
    per_main = 2 + sides

    def kernel(base_ref, *refs):
        main_refs, skip_refs = refs[: len(main)], refs[len(main) : len(main) + len(skip)]
        w_skip, w_attn, w_up, w_down, s_main, s_skip = refs[len(main) + len(skip) :]
        is_dec, quarter, rank = base_ref[0] == 1, base_ref[8], base_ref[9]
        which = [quarter, quarter ^ 1, jnp.where(is_dec, 1, 2), jnp.where(is_dec, 0, 3)]

        def rows_of(index, count):
            shard = which[index % 4] * span + (rank ^ (index // 4))
            return pl.multiple_of(shard * count, count)

        @pl.when(base_ref[7] == 0)
        def _():
            copies, skip_copies = [], []
            for index, source in enumerate(skip_refs):
                count = source.shape[0]
                target = w_skip.at[pl.ds(rows_of(index, count), count)]
                skip_copies.append(pltpu.make_async_copy(source, target, s_skip.at[index]))
            for index, source in enumerate(main_refs):
                count = source.shape[1]
                start = rows_of(index, count)
                sems = s_main.at[index]
                for place, whole in enumerate((w_attn, w_up)):
                    target = whole.at[pl.ds(start, count)]
                    copies.append(pltpu.make_async_copy(source.at[place], target, sems.at[place]))
                for side in range(sides):
                    block = source.at[2, :, pl.ds(side * width, width)]
                    row = pl.multiple_of(start * sides + side * count, count)
                    target = w_down.at[pl.ds(row, count)]
                    copies.append(pltpu.make_async_copy(block, target, sems.at[2 + side]))

            @pl.when(is_dec)
            def _():
                for copy in skip_copies:
                    copy.start()

            for copy in copies:
                copy.start()
            for copy in copies:
                copy.wait()

            @pl.when(is_dec)
            def _():
                for copy in skip_copies:
                    copy.wait()

    return list(
        pl.pallas_call(
            kernel,
            out_shape=[
                pltpu.VMEM((2 * width, width), BF16),
                pltpu.VMEM((width, 4 * width), BF16),
                pltpu.VMEM((width, hidden_size), BF16),
                pltpu.VMEM((hidden_size, width), BF16),
            ],
            in_specs=[IN_SMEM] + [IN_HBM] * (len(main) + len(skip)),
            out_specs=[IN_VMEM] * 4,
            scratch_shapes=[
                pltpu.SemaphoreType.DMA((len(main), per_main)),
                pltpu.SemaphoreType.DMA((len(skip),)),
            ],
            compiler_params=pltpu.CompilerParams(vmem_limit_bytes=VMEM_LIMIT),
            cost_estimate=QUICK,
            name="assemble",
        )(base, *(stay_in_hbm(part) for part in main + skip))
    )


def weight_products(base, first, slots_used, span, specs, lefts, rights, came, earlier):
    names_left, names_right = list(lefts), list(rights)
    direct = {name: lefts[name].ndim == 3 for name in names_left}
    units = []
    for matrix, (rows, cols, blocks) in enumerate(specs):
        quads = [tuple(range(4))] if 4 * rows <= 512 else [(q,) for q in range(4)]
        for left, right, source, column, size in blocks:
            for quad in quads:
                units.append((matrix, quad, rows, left, right, source, column, size))
    steps = [(other, unit) for other in (range(1, span) if first else (0,)) for unit in units]
    left_width = max(-(-len(quad) * rows // 128) * 128 for _, quad, rows, *_ in units)
    right_width = max(unit[7] for unit in units)
    side_cols = max(cols for _, cols, _ in specs)
    side_rows = min(rows for rows, _, _ in specs)
    outs = []
    if first:
        for rows, cols, _ in specs:
            outs += [pltpu.HBM((4, rows, cols), BF16)] * (span - 1)
    else:
        outs += [pltpu.HBM((len(specs), side_rows, side_cols), BF16)] * 3
        outs += [pltpu.HBM((rows, cols), F32) for rows, cols, _ in specs]
        outs += [pltpu.HBM((8, right_width), F32)]
    n_in = len(names_left) + len(names_right)
    n_came = len(came)

    def kernel(base_ref, *refs):
        left_refs = dict(zip(names_left, refs))
        right_refs = dict(zip(names_right, refs[len(names_left) :]))
        came_refs = refs[n_in : n_in + n_came]
        at = n_in + n_came + len(earlier)
        out_refs = refs[at : at + len(outs)]
        x_buf, y_buf, came_buf, low_buf, own_buf, sum_buf, s_x, s_y, s_came, s_out = refs[
            at + len(outs) :
        ]
        is_dec, rank = base_ref[0], base_ref[9]
        edge = jnp.where(is_dec == 1, 3, 0)
        own = jnp.where(is_dec == 1, 2, 1)
        near, far = jnp.where(is_dec == 1, 1, 2), jnp.where(is_dec == 1, 0, 3)

        def loads(index):
            other, (matrix, quad, rows, left, right, source, column, size) = steps[index]
            slot = index % 2
            copies = []
            for place, q in enumerate(quad):
                if direct[left]:
                    start = pl.multiple_of((q * span + (rank ^ other)) * rows, 128)
                    block = left_refs[left].at[pl.ds(0, slots_used), :, pl.ds(start, rows)]
                    target = x_buf.at[slot, :, :, pl.ds(place * rows, rows)]
                elif place == 0:
                    block = left_refs[left].at[rank ^ other, pl.ds(0, slots_used)]
                    target = x_buf.at[slot, :, :, pl.ds(0, lefts[left].shape[3])]
                else:
                    continue
                copies.append((block, target, s_x.at[slot, place]))
            block = right_refs[right].at[pl.ds(0, slots_used), :, pl.ds(source, size)]
            copies.append((block, y_buf.at[slot, :, :, pl.ds(0, size)], s_y.at[slot]))
            return [pltpu.make_async_copy(*copy) for copy in copies]

        def add_loads(index):
            _, (matrix, quad, rows, left, right, source, column, size) = steps[index]
            count = len(quad)
            copies = []
            for other in range(n_came // len(specs)):
                block = came_refs[matrix * (span - 1) + other].at[
                    pl.ds(quad[0], count), :, pl.ds(column, size)
                ]
                target = came_buf.at[other, pl.ds(0, count), pl.ds(0, rows), pl.ds(0, size)]
                copies.append(pltpu.make_async_copy(block, target, s_came.at[other]))
            return copies

        def run():
            for copy in loads(0):
                copy.start()
            sum_buf[...] = jnp.zeros(sum_buf.shape, F32)
            pending = {0: [], 1: []}
            for index, (other, unit) in enumerate(steps):
                matrix, quad, rows, left, right, source, column, size = unit
                slot, count = index % 2, len(quad)
                if index + 1 < len(steps):
                    for copy in loads(index + 1):
                        copy.start()
                adds = [] if first else add_loads(index)
                for copy in adds:
                    copy.start()
                for copy in loads(index):
                    copy.wait()
                deep = slots_used * x_buf.shape[2]
                x = x_buf[slot, :, :, : count * rows].reshape(deep, count * rows)
                y = y_buf[slot, :, :, :size].reshape(deep, size)
                total = matmul_tn(x, y).reshape(count, rows, size)
                for copy in adds:
                    copy.wait()
                for which in range(len(adds)):
                    total = total + came_buf[which, :count, :rows, :size].astype(F32)
                for copy in pending[slot]:
                    copy()
                pending[slot] = []
                low_buf[slot, :count, :rows, :size] = to_low(total)

                def send(block, target, sem, condition=None):
                    copy = pltpu.make_async_copy(block, target, sem)
                    if condition is None:
                        copy.start()
                        pending[slot].append(copy.wait)
                        return

                    @pl.when(condition)
                    def _():
                        copy.start()

                    def wait():
                        @pl.when(condition)
                        def _():
                            copy.wait()

                    pending[slot].append(wait)

                staged = low_buf.at[slot, :, pl.ds(0, rows), pl.ds(0, size)]
                wide = own_buf.at[slot, pl.ds(0, rows), pl.ds(0, size)]
                cut = pl.ds(column, size)
                if first:
                    send(
                        staged.at[pl.ds(0, count)],
                        out_refs[matrix * (span - 1) + other - 1].at[pl.ds(quad[0], count), :, cut],
                        s_out.at[slot, 0, 0],
                    )
                    continue
                parts = rows // side_rows
                for place, whose in enumerate((edge, near, far)):
                    for part in range(parts):
                        target = out_refs[place].at[
                            matrix, :, pl.ds(part * side_cols // parts + column, size)
                        ]
                        source = staged.at[
                            whose if count == 4 else 0, pl.ds(part * side_rows, side_rows)
                        ]
                        condition = None if count == 4 else whose == quad[0]
                        send(source, target, s_out.at[slot, place, part], condition)
                for place, q in enumerate(quad):

                    @pl.when(own == q)
                    def _():
                        own_buf[slot, :rows, :size] = total[place]
                        squares = (total[place] * total[place]).reshape(-1, 8, size)
                        sum_buf[:, :size] += jnp.sum(squares, axis=0)

                condition = None if count == 4 else own == quad[0]
                send(wide, out_refs[3 + matrix].at[:, cut], s_out.at[slot, 3, 0], condition)
            for slot in (0, 1):
                for copy in pending[slot]:
                    copy()
            if not first:
                copy = pltpu.make_async_copy(sum_buf, out_refs[-1], s_y.at[0])
                copy.start()
                copy.wait()

        pl.when(base_ref[7] == 0)(run)

    row_len = rights[names_right[0]].shape[1]
    tall = max(rows for rows, _, _ in specs)
    quad_rows = max(len(quad) for _, quad, *_ in units)
    results = pl.pallas_call(
        kernel,
        out_shape=outs,
        in_specs=[IN_SMEM] + [IN_HBM] * (n_in + n_came + len(earlier)),
        out_specs=[IN_HBM] * len(outs),
        scratch_shapes=[
            pltpu.VMEM((2, slots_used, row_len, left_width), BF16),
            pltpu.VMEM((2, slots_used, row_len, right_width), BF16),
            pltpu.VMEM((max(n_came // len(specs), 1), quad_rows, tall, right_width), BF16),
            pltpu.VMEM((2, quad_rows, tall, right_width), BF16),
            pltpu.VMEM((2, tall, right_width), F32),
            pltpu.VMEM((8, right_width), F32),
            pltpu.SemaphoreType.DMA((2, 4)),
            pltpu.SemaphoreType.DMA((2,)),
            pltpu.SemaphoreType.DMA((max(span - 1, 1),)),
            pltpu.SemaphoreType.DMA((2, 4, tall // side_rows)),
        ],
        compiler_params=pltpu.CompilerParams(vmem_limit_bytes=2 * VMEM_LIMIT),
        cost_estimate=QUICK,
        name="weight_products",
    )(base, *(stay_in_hbm(a) for a in (*lefts.values(), *rights.values(), *came, *earlier)))
    return list(results)


def adam_update(master, first, second, gradient, factor, step_rate):
    gradient = gradient * factor
    first_new = beta_one * first + (1.0 - beta_one) * gradient
    second_new = beta_two * second + (1.0 - beta_two) * gradient * gradient
    corrected = first_new / (1.0 - beta_one**STEP)
    spread = jnp.sqrt(second_new / (1.0 - beta_two**STEP))
    master_new = master - step_rate * (corrected / (spread + adam_eps) + weight_decay * master)
    return (master_new, first_new, second_new, master_new.astype(BF16))


def body(
    clean_mel,
    noise,
    phone_ids,
    segment_ids,
    loss_mask,
    time_idx,
    attn_w,
    attn_m,
    attn_v,
    up_w,
    up_m,
    up_v,
    down_w,
    down_m,
    down_v,
    skip_w,
    skip_m,
    skip_v,
    gain_w,
    gain_m,
    gain_v,
    table_w,
    table_m,
    table_v,
):
    sections = lax.axis_size("section")
    batch = lax.axis_size("batch")
    section_id = lax.axis_index("section")
    batch_id = lax.axis_index("batch")
    span = batch // 4
    quarter, rank = batch_id // span, batch_id % span
    is_dec = quarter >= 2
    is_outer = (quarter == 0) | (quarter == 3)
    local_rows, row_len, mel_bins = clean_mel.shape
    width = attn_w.shape[3] // 4
    hidden_size = up_w.shape[3]
    total_rows = local_rows * batch
    slots = total_rows // span
    top = 2 * sections - 1
    pos = jnp.where(is_dec, top - section_id, section_id)
    chain_rows = jnp.where(is_outer, 0, slots)
    base = jnp.stack(
        [is_dec, section_id, pos, 0, chain_rows, slots, top, is_outer, quarter, rank]
    ).astype(jnp.int32)

    near, far, back_far = ((1, 2), (2, 1)), ((0, 2), (3, 1)), ((1, 3), (2, 0))
    inward, outward = ((0, 1), (3, 2)), ((1, 0), (2, 3))

    def along(block, pairs):
        route = [(a * span + i, b * span + i) for a, b in pairs for i in range(span)]
        return lax.ppermute(block, "batch", route)

    def across(block, bits, members=(0, 1, 2, 3)):
        route = [(a * span + i, a * span + (i ^ bits)) for a in members for i in range(span)]
        return lax.ppermute(block, "batch", route)

    def flipped(block, axis, bit):
        return lax.ppermute(block, axis, [(i, i ^ bit) for i in range(lax.axis_size(axis))])

    def at_stage(stage):
        return (stage, 1) if stage < sections else (top - stage, 2)

    def stage_route(pairs):
        route = []
        for source, target in pairs:
            (s, a), (t, b) = at_stage(source), at_stage(target)
            route += [(s * batch + a * span + i, t * batch + b * span + i) for i in range(span)]
        return route

    chain_forward = stage_route([(stage, stage + 1) for stage in range(top)])
    chain_backward = stage_route([(stage + 1, stage) for stage in range(top)])
    skip_forward = stage_route([(s, top - s) for s in range(sections - 1)])
    skip_backward = stage_route([(top - s, s) for s in range(sections - 1)])

    times = jnp.stack([time_idx // 32, time_idx % 32], axis=1)
    small = [
        clean_mel.reshape(-1),
        noise.reshape(-1),
        to_low(jnp.stack([phone_ids, segment_ids, loss_mask], axis=1)).reshape(-1),
        to_low(times).reshape(-1),
        to_low(gain_w[0]).reshape(-1),
    ]
    sizes = [part.size for part in small]
    packed = jnp.pad(jnp.concatenate(small), (0, -sum(sizes) % 1024)).reshape(1, -1, 128)
    everyone = lax.all_gather(packed, "batch", axis=0, tiled=True).reshape(batch, -1)
    parts = []
    offset = 0
    for size in sizes:
        parts.append(everyone[:, offset : offset + size])
        offset += size

    def every_rank(piece, members):
        return [piece] + [across(piece, bits, members) for bits in range(1, span)]

    def gather_shards(enc_part, dec_part, only_dec):
        limit = (lambda pairs: tuple(p for p in pairs if p[1] >= 2)) if only_dec else (lambda p: p)
        members = (2,) if only_dec else (1, 2)
        own = ordered(jnp.where(is_dec, dec_part, enc_part), everyone)
        other = ordered(jnp.where(is_dec, enc_part, dec_part), everyone)
        pieces = (
            own,
            along(own, limit(inward)),
            along(other, limit(near)),
            along(other, limit(far)),
        )
        return [list(group) for group in zip(*(every_rank(p, members) for p in pieces))]

    def packed_shard(layer):
        rows = width // batch
        down = to_low(down_w[0, layer])
        side = [down[i * rows : (i + 1) * rows] for i in range(hidden_size // width)]
        return jnp.stack(
            [to_low(attn_w[0, layer]), to_low(up_w[0, layer]), jnp.concatenate(side, axis=1)]
        )

    skip_low = to_low(skip_w[0])
    skip_shards = gather_shards(skip_low, skip_low, True)
    main_shards = gather_shards(packed_shard(0), packed_shard(1), False)
    weights = assemble(base, main_shards, skip_shards, span, width, hidden_size)

    all_clean = parts[0].reshape(total_rows, row_len, mel_bins)
    all_noise = parts[1].reshape(total_rows, row_len, mel_bins)
    all_ids = parts[2].reshape(total_rows, 3, row_len).astype(F32)
    all_times = parts[3].reshape(total_rows, 2).astype(F32)
    all_gains = parts[4].reshape(batch, 4, width // batch)
    all_gains = jnp.moveaxis(all_gains, 0, 1).reshape(4, width).astype(F32)
    gains = jnp.where(is_dec, all_gains[2:4], all_gains[0:2])
    mask_total = jnp.sum(all_ids[:, 2])

    def chain_part(array):
        return lax.dynamic_slice_in_dim(array, rank * slots, slots, 0)

    clean_rows = chain_part(all_clean).astype(F32)
    noise_rows = chain_part(all_noise).astype(F32)
    ids = chain_part(all_ids)
    time_parts = chain_part(all_times)
    phones, segments, weight = ids[:, 0], ids[:, 1], ids[:, 2]
    flow_time = (time_parts[:, 0] * 32.0 + time_parts[:, 1]) / TSTEPS
    wide_time = flow_time[:, None, None]
    noisy_mel = (1.0 - (1.0 - sigma_min) * wide_time) * noise_rows + wide_time * clean_rows
    context_mel = clean_rows * (1.0 - weight)[..., None]
    target = clean_rows - (1.0 - sigma_min) * noise_rows
    onehot = to_low(phones[..., None] == jnp.arange(VOCAB, dtype=F32))
    front = jnp.concatenate([to_low(noisy_mel), to_low(context_mel), onehot], axis=2)
    half = width // 2
    frequency = jnp.exp(-math.log(10000.0) * jnp.arange(half, dtype=F32) / half) * (
        1000.0 * flow_time[:, None]
    )
    timing = jnp.concatenate([jnp.sin(frequency), jnp.cos(frequency)], axis=1)
    table_low = to_low(table_w)
    front_rows = 2 * mel_bins + VOCAB
    head_rows = table_low[front_rows : front_rows + mel_bins]
    out_gain = table_low[front_rows + mel_bins].astype(F32)[None]
    flat_front = front.reshape(slots * row_len, front_rows)
    embedded = (
        matmul(flat_front[:, : 2 * mel_bins], table_low[: 2 * mel_bins])
        + matmul(flat_front[:, 2 * mel_bins :], table_low[2 * mel_bins : front_rows])
    ).reshape(slots, row_len, width)
    embedded = to_low(embedded + timing[:, None, :])
    allowed = (segments[:, :, None] == segments[:, None, :]).astype(F32)
    frame_weight = jnp.broadcast_to(weight[..., None], (slots, row_len, 128))
    target = jnp.pad(target, ((0, 0), (0, 0), (0, 128 - mel_bins)))
    head_rows = jnp.pad(head_rows, ((0, 128 - mel_bins), (0, 0)))
    scale = (2.0 / (mel_bins * mask_total))[None]
    base, embedded, allowed, frame_weight, target, head_rows, out_gain, scale, flat_front = (
        lax.optimization_barrier(
            (base, embedded, allowed, frame_weight, target, head_rows, out_gain, scale, flat_front)
        )
    )
    embedded, allowed = stay_in_hbm(embedded), stay_in_hbm(allowed)

    kept = unwritten(kept_shapes(slots, row_len, width, hidden_size))
    transposed = unwritten(transposed_shapes(weights))
    blank = jnp.zeros((row_len, width), BF16)
    waits = [LAG * (top - 2 * s) for s in range(sections - 1)]
    soon = 2 * LAG
    tick_count = LAG * top + slots
    skip_sent, arriving = [], []
    for tick in range(tick_count):
        arrived = arriving[tick - LAG] if tick >= LAG else blank
        skips = [skip_sent[tick - wait] if tick >= wait else blank for wait in waits]
        in_flight = skip_sent[tick - soon] if tick >= soon else blank
        for for_dec, begin in ((True, 0), (False, LAG * (sections - 1) + slots - 2)):
            which, half = (tick - begin) // 2, (tick - begin) % 2
            if tick in range(begin, begin + 2 * len(weights)) and (for_dec or which):
                weights[which], transposed[which] = transpose_half(
                    base, weights[which], transposed[which], half, for_dec
                )
        output, kept, weights = forward_tick(
            base, tick, arrived, embedded, skips, allowed, in_flight, gains, weights, kept
        )
        arriving.append(lax.ppermute(output, BOTH, chain_forward))
        is_needed = tick < LAG * (sections - 2) + slots
        skip_sent.append(lax.ppermute(output, BOTH, skip_forward) if is_needed else blank)

    head_grads, head_total, out_gain_total, loss_parts, *weights = head_pass(
        base, kept[10], target, frame_weight, head_rows, out_gain, scale, mel_bins, transposed
    )

    head_grads = stay_in_hbm(head_grads)

    grads = unwritten(grad_shapes(slots, row_len, width, hidden_size))
    skip_sent, arriving = [], []
    for tick in range(tick_count):
        arrived = arriving[tick - LAG] if tick >= LAG else blank
        skips = [skip_sent[tick - wait] if tick >= wait else blank for wait in waits]
        in_flight = skip_sent[tick - soon] if tick >= soon else blank
        output, skip_output, grads, weights = backward_tick(
            base, tick, arrived, head_grads, skips, in_flight, gains, weights, kept, grads
        )
        arriving.append(lax.ppermute(output, BOTH, chain_backward))
        is_needed = tick < LAG * (sections - 2) + slots
        skip_sent.append(lax.ppermute(skip_output, BOTH, skip_backward) if is_needed else blank)

    columns = min(1024, width)
    attn_blocks = [
        ("ain", "qkvg", start, start, columns) for start in range(0, 3 * width, columns)
    ] + [("ctx", "proj", start, 3 * width + start, columns) for start in range(0, width, columns)]
    specs = {
        "down": (
            hidden_size // batch,
            width,
            [("act", "branch", start, start, columns) for start in range(0, width, columns)],
        ),
        "up": (
            width // batch,
            hidden_size,
            [("fin", "hid", start, start, columns) for start in range(0, hidden_size, columns)],
        ),
        "attn": (width // batch, 4 * width, attn_blocks),
        "skip": (
            2 * width // batch,
            width,
            [("join", "resg", start, start, columns) for start in range(0, width, columns)],
        ),
    }
    lefts = dict(zip(("join", "ain", "ctx", "fin", "act"), (kept[i] for i in (0, 2, 5, 7, 8))))
    rights = dict(zip(("branch", "hid", "proj", "qkvg", "resg"), grads))

    def lefts_of(name):
        rows = specs[name][0]
        found = {}
        for left in dict.fromkeys(block[0] for block in specs[name][2]):
            array = lefts[left]
            if rows % 128:
                array = array.reshape(slots, row_len, 4, span, rows)
                array = jnp.moveaxis(array, 3, 0).reshape(span, slots, row_len, 4 * rows)
                array = jnp.pad(array, ((0, 0),) * 3 + ((0, -4 * rows % 128),))
            found[left] = array
        return found

    def products(names, first, came, earlier):
        wanted = dict.fromkeys(block[1] for name in names for block in specs[name][2])
        found = {}
        for name in names:
            found |= lefts_of(name)
        return weight_products(
            base,
            first,
            slots,
            span,
            [specs[name] for name in names],
            found,
            {right: rights[right] for right in wanted},
            came,
            [stay_in_hbm(array) for array in earlier],
        )

    groups = (("skip",), ("up", "down", "attn"))
    came, own_grads, arrived_grads, own_squares = {}, {}, {}, {}
    earlier = []
    for names in groups:
        sent = products(names, True, [], earlier)
        if not earlier:
            table_earlier = sent[0]
        earlier = sent[:1]
        members = (2,) if names == ("skip",) else (1, 2)
        bits = [1 + i % (span - 1) for i in range(len(sent))]
        came[names] = [across(part, bit, members) for part, bit in zip(sent, bits)]

    for names in groups:
        results = products(names, False, came[names], earlier)
        earlier = results[:1]
        limit = (
            (lambda pairs: tuple(p for p in pairs if p[0] >= 2))
            if names == ("skip",)
            else (lambda pairs: pairs)
        )
        arrived_grads[names] = [
            along(part, limit(pairs)) for part, pairs in zip(results, (outward, near, back_far))
        ]
        own_grads |= dict(zip(names, results[3:-1]))
        own_squares[names] = results[-1]

    table_count = front_rows + mel_bins + 1
    table_rows = -(-table_count // (16 * span)) * 16 * span
    shared = table_pass(
        base, flat_front, grads[4], grads[5], head_total, out_gain_total, table_rows, table_earlier
    )
    bit = 1
    while bit < span:
        shared = shared + across(shared, bit)
        bit *= 2
    share = table_rows // span
    mine = lax.dynamic_slice_in_dim(shared, rank * share, share, 0)
    first_rank = (rank == 0) & ~is_outer
    small_squares = jnp.sum(mine.astype(F32) ** 2) + jnp.where(
        first_rank, jnp.sum(shared[table_rows:].astype(F32) ** 2), 0.0
    )
    mine = jnp.concatenate([mine, shared[table_rows:]])
    mine = mine + along(mine, near)
    mine = mine + along(mine, outward)
    gain_rows = mine[share : share + 4].astype(F32)
    mine = mine[:share]
    bit = 1
    while bit < sections:
        mine = mine + flipped(mine, "section", bit)
        bit *= 2
    table_parts = [mine] + [across(mine, bits) for bits in range(1, span)]
    table_grad = jnp.zeros((table_rows, width), BF16)
    for bits, part in enumerate(table_parts):
        table_grad = lax.dynamic_update_slice_in_dim(table_grad, part, (rank ^ bits) * share, 0)
    gain_grad = lax.dynamic_slice_in_dim(
        gain_rows, batch_id * (width // batch), width // batch, 1
    )


    def squares_of(names):
        edge, close, distant = (part.astype(F32) for part in arrived_grads[names])
        inner = jnp.sum(own_squares[names])
        own = jnp.where(is_outer, jnp.sum(edge**2), inner)
        other = jnp.where(is_outer, jnp.sum(distant**2), jnp.sum(close**2))
        return jnp.where(is_dec, own, other) if names == ("skip",) else own + other

    squares = sum(squares_of(names) for names in groups) + small_squares
    loss_local = jnp.where(is_outer, 0.0, jnp.sum(loss_parts))
    lane = lax.broadcasted_iota(jnp.int32, (8, 128), 1)
    sums = jnp.where(lane == 0, squares, jnp.where(lane == 1, loss_local, 0.0))
    for axis, size in (("batch", batch), ("section", sections)):
        bit = 1
        while bit < size:
            sums = sums + flipped(sums, axis, bit)
            bit *= 2
    loss_sum = sums[0, 1]
    grad_norm = jnp.sqrt(sums[0, 0])
    factor = clip_norm / jnp.maximum(grad_norm, clip_norm)

    def both_layers(name):
        index = groups[1].index(name)
        edge, close, distant = (part[index] for part in arrived_grads[groups[1]])
        if name == "down":
            edge, close, distant = (
                jnp.concatenate(
                    [part[:, i * width : (i + 1) * width] for i in range(hidden_size // width)]
                )
                for part in (edge, close, distant)
            )
        own = jnp.where(is_outer, edge.astype(F32), own_grads[name])
        other = jnp.where(is_outer, distant, close).astype(F32)
        return jnp.stack([jnp.where(is_dec, other, own), jnp.where(is_dec, own, other)])[None]

    attn_out = adam_update(attn_w, attn_m, attn_v, both_layers("attn"), factor, rate_matrix)
    up_out = adam_update(up_w, up_m, up_v, both_layers("up"), factor, rate_matrix)
    down_out = adam_update(down_w, down_m, down_v, both_layers("down"), factor, rate_matrix)
    edge, close, distant = (part[0].astype(F32) for part in arrived_grads[groups[0]])
    skip_grad = jnp.where(
        is_dec, jnp.where(is_outer, edge, own_grads["skip"]), jnp.where(is_outer, distant, close)
    )
    skip_out = adam_update(skip_w, skip_m, skip_v, skip_grad[None], factor, rate_matrix)
    table_grad = table_grad[:table_count].astype(F32)
    gain_out = adam_update(gain_w, gain_m, gain_v, gain_grad[None], factor, rate_gain)
    table_out = adam_update(table_w, table_m, table_v, table_grad, factor, rate_table)
    return (
        loss_sum, mask_total, grad_norm,
        *attn_out, *up_out, *down_out, *skip_out, *gain_out, *table_out,
    )


def solution(mesh):
    row_specs = (
        P("batch", None, None),
        P("batch", None, None),
        P("batch", None),
        P("batch", None),
        P("batch", None),
        P("batch"),
    )
    wide = P("section", None, "batch", None)
    flat = P("section", "batch", None)
    gain = P("section", None, "batch")
    return jax.shard_map(
        body,
        mesh=mesh,
        in_specs=row_specs + (wide,) * 9 + (flat,) * 3 + (gain,) * 3 + (P(),) * 3,
        out_specs=(P(),) * 3 + (wide,) * 12 + (flat,) * 4 + (gain,) * 4 + (P(),) * 4,
        check_vma=False,
    )
```

```python
import math

import jax
import jax.numpy as jnp
from jax import lax
from jax.experimental import pallas as pl
from jax.experimental.pallas import tpu as pltpu
from jax.sharding import PartitionSpec as P

HEADS = 16
VOCAB = 256
TSTEPS = 1000
STEP = 10

norm_eps = 1e-05
beta_one = 0.9
beta_two = 0.999
adam_eps = 1e-08
rate_matrix = 0.02
rate_gain = 0.5
rate_table = 0.25
weight_decay = 0.01
clip_norm = 0.005
sigma_min = 1e-05

LAG = 2
BOTH = ("section", "batch")
BF16 = jnp.bfloat16
F32 = jnp.float32
BLOCK = 1024
SLOPES = [2.0 ** (-8.0 * (head + 1) / HEADS) for head in range(HEADS)]
VMEM_LIMIT = 16 * 2**20
QUICK = pl.CostEstimate(flops=1, bytes_accessed=1, transcendentals=0)


def to_low(operand):
    return operand.astype(BF16)


def matmul(left, right):
    return jnp.dot(left, right, preferred_element_type=F32)


def matmul_nt(left, right):
    return lax.dot_general(left, right, (((1,), (1,)), ((), ())), preferred_element_type=F32)


def matmul_tn(left, right):
    return lax.dot_general(left, right, (((0,), (0,)), ((), ())), preferred_element_type=F32)


def normalize(operand, gain):
    centered = operand - jnp.mean(operand, axis=-1, keepdims=True)
    variance = jnp.mean(centered * centered, axis=-1, keepdims=True)
    return centered * lax.rsqrt(variance + norm_eps) * gain


def normalize_back(grad, operand, gain):
    centered = operand - jnp.mean(operand, axis=-1, keepdims=True)
    scale = lax.rsqrt(jnp.mean(centered * centered, axis=-1, keepdims=True) + norm_eps)
    unit = centered * scale
    scaled = grad * gain
    along = jnp.mean(scaled * unit, axis=-1, keepdims=True)
    back = scale * (scaled - jnp.mean(scaled, axis=-1, keepdims=True) - unit * along)
    return back, jnp.sum(grad * unit, axis=0, keepdims=True)


def head_masks(rows):
    lanes = lax.broadcasted_iota(jnp.int32, (rows, 128), 1)
    return lanes < 64


def split_heads(slab, low_half):
    zero = jnp.zeros_like(slab)
    return jnp.concatenate(
        [jnp.where(low_half, slab, zero), jnp.where(low_half, zero, slab)], axis=0
    )


def live_slot(base, tick, steps_before):
    lag_count = tick - steps_before
    return (lag_count >= 0) & (lag_count < base[4]), jnp.clip(lag_count, 0, base[5] - 1)


def forward_kernel(
    base, tick_ref, arrived, embedded, skip_a, skip_b, skip_c, allowed, in_flight, gains,
    w_skip, w_attn, w_up, w_down,
    in_join, in_res, in_ain, in_qkv, in_prob, in_ctx, in_mid, in_fin, in_act, in_slope, in_final,
    leaving, o_join, o_res, o_ain, o_qkv, o_prob, o_ctx, o_mid, o_fin, o_act, o_slope, o_final,
    same_skip, same_attn, same_up, same_down,
    join, allow, res, ain, qkv, prob, ctx, mid, fin, act, slope, sent, acc, sem_in, sem_out,
):
    is_dec, pair, pos = base[0], base[1], base[2]
    is_live, slot = live_slot(base, tick_ref[0], LAG * pos + base[3])
    rows, width = res.shape
    hidden_size = act.shape[1]

    @pl.when(is_live)
    def _():
        first_half = join.at[:, pl.ds(0, width)]
        second_half = join.at[:, pl.ds(width, width)]
        from_rows = pltpu.make_async_copy(embedded.at[slot], first_half, sem_in.at[0])
        from_chain = pltpu.make_async_copy(arrived, first_half, sem_in.at[0])
        mask_copy = pltpu.make_async_copy(allowed.at[slot], allow, sem_in.at[2])
        skips = [
            pltpu.make_async_copy(source, second_half, sem_in.at[1])
            for source in (skip_a, skip_b, skip_c, arrived)
        ]

        @pl.when(pos == 0)
        def _():
            from_rows.start()

        @pl.when(pos != 0)
        def _():
            from_chain.start()

        @pl.when(is_dec == 1)
        def _():
            for which in range(4):

                @pl.when(pair == which)
                def _():
                    skips[which].start()

        mask_copy.start()
        from_chain.wait()
        outgoing = []

        def keep(source, target, index):
            copy = pltpu.make_async_copy(source, target.at[slot], sem_out.at[index])
            copy.start()
            outgoing.append(copy)

        @pl.when(is_dec == 1)
        def _():
            skips[0].wait()
            for start in range(0, width, BLOCK):
                cut = slice(start, start + BLOCK)
                res[:, cut] = matmul(join[...], w_skip[:, cut])

        @pl.when(is_dec == 0)
        def _():
            res[...] = join[:, :width].astype(F32)

        keep(join, o_join, 0)
        keep(res, o_res, 1)
        ain[...] = to_low(normalize(res[...], gains[0:1, :]))
        keep(ain, o_ain, 2)
        for start in range(0, 3 * width, BLOCK):
            cut = slice(start, start + BLOCK)
            qkv[:, cut] = to_low(matmul(ain[...], w_attn[:, cut]))
        keep(qkv, o_qkv, 3)
        mask_copy.wait()
        row_ids = lax.broadcasted_iota(jnp.int32, (rows, rows), 0)
        col_ids = lax.broadcasted_iota(jnp.int32, (rows, rows), 1)
        distance = jnp.abs(row_ids - col_ids).astype(F32)
        is_allowed = allow[...] > 0.5
        low_half = head_masks(rows)
        for two in range(HEADS // 2):
            cut = slice(two * 128, two * 128 + 128)
            queries = split_heads(qkv[:, cut], low_half)
            keys = qkv[:, width + two * 128 : width + two * 128 + 128]
            scores = matmul_nt(queries, keys) * 0.125
            prob[2 * two] = scores[:rows]
            prob[2 * two + 1] = scores[rows:]
        for head in range(HEADS):
            scores = jnp.where(is_allowed, prob[head] + (-SLOPES[head]) * distance, -1e30)
            powers = jnp.exp(scores - jnp.max(scores, axis=-1, keepdims=True))
            prob[head] = powers * (1.0 / jnp.sum(powers, axis=-1, keepdims=True))
        for two in range(HEADS // 2):
            cut = slice(two * 128, two * 128 + 128)
            values = qkv[:, 2 * width + two * 128 : 2 * width + two * 128 + 128]
            chances = jnp.concatenate([to_low(prob[2 * two]), to_low(prob[2 * two + 1])], axis=0)
            mixed = matmul(chances, values)
            ctx[:, cut] = to_low(jnp.where(low_half, mixed[:rows], mixed[rows:]))
        keep(prob, o_prob, 4)
        keep(ctx, o_ctx, 5)
        for start in range(0, width, BLOCK):
            cut = slice(start, start + BLOCK)
            column = 3 * width + start
            mid[:, cut] = res[:, cut] + matmul(ctx[...], w_attn[:, column : column + BLOCK])
        keep(mid, o_mid, 6)
        fin[...] = to_low(normalize(mid[...], gains[1:2, :]))
        keep(fin, o_fin, 7)
        for start in range(0, hidden_size, BLOCK):
            cut = slice(start, start + BLOCK)
            hidden = matmul(fin[...], w_up[:, cut])
            below = 0.5 + 0.5 * lax.erf(hidden * (2.0**-0.5))
            density = (2.0 * math.pi) ** -0.5 * jnp.exp(-0.5 * hidden * hidden)
            act[:, cut] = to_low(hidden * below)
            slope[:, cut] = to_low(below + hidden * density)
            part = matmul(act[:, cut], w_down[cut, :])
            if start == 0:
                acc[...] = part
            else:
                acc[...] += part
        keep(act, o_act, 8)
        keep(slope, o_slope, 9)
        sent[...] = to_low(mid[...] + acc[...])

        @pl.when(pos == base[6])
        def _():
            last = pltpu.make_async_copy(sent, o_final.at[slot], sem_in.at[1])
            last.start()
            last.wait()

        leave = pltpu.make_async_copy(sent, leaving, sem_in.at[0])
        leave.start()
        leave.wait()
        for copy in outgoing:
            copy.wait()


def backward_kernel(
    base, tick_ref, arrived, head_grads, skip_a, skip_b, skip_c, in_flight, gains,
    w_skip, w_attn, w_up, w_down, k_res, k_qkv, k_prob, k_mid, k_slope,
    in_branch, in_hid, in_proj, in_qkvg, in_resg, in_gain,
    leaving, leaving_skip, o_branch, o_hid, o_proj, o_qkvg, o_resg, o_gain,
    same_skip, same_attn, same_up, same_down,
    x_low, x_wide, x_skip, res, qkv, prob, mid, slope, grad, branch, hid, proj, qkvg, resg, gain_g,
    acc, ctx_g, joined, sem_in, sem_out,
):
    is_dec, pair, pos = base[0], base[1], base[2]
    is_live, slot = live_slot(base, tick_ref[0], LAG * (base[6] - pos))
    is_last = pos == base[6]
    rows, width = res.shape
    hidden_size = hid.shape[1]

    @pl.when(is_live)
    def _():
        from_head = pltpu.make_async_copy(head_grads.at[slot], x_wide, sem_in.at[0])
        from_chain = pltpu.make_async_copy(arrived, x_low, sem_in.at[1])
        skips = [
            pltpu.make_async_copy(source, x_skip, sem_in.at[2])
            for source in (skip_a, skip_b, skip_c)
        ]
        kept = [
            pltpu.make_async_copy(source.at[slot], target, sem_in.at[3 + index])
            for index, (source, target) in enumerate(
                ((k_slope, slope), (k_mid, mid), (k_prob, prob), (k_qkv, qkv), (k_res, res))
            )
        ]
        with_skip = (is_dec == 0) & (pair < 3)

        @pl.when(is_last)
        def _():
            from_head.start()

        @pl.when(jnp.logical_not(is_last))
        def _():
            from_chain.start()

        @pl.when(with_skip)
        def _():
            for which in range(3):

                @pl.when(pair == which)
                def _():
                    skips[which].start()

        for copy in kept:
            copy.start()
        outgoing = []

        def keep(source, target, index):
            copy = pltpu.make_async_copy(source, target.at[slot], sem_out.at[index])
            copy.start()
            outgoing.append(copy)

        @pl.when(is_last)
        def _():
            from_head.wait()
            grad[...] = x_wide[...]

        @pl.when(jnp.logical_not(is_last))
        def _():
            from_chain.wait()
            grad[...] = x_low[...].astype(F32)

        @pl.when(with_skip)
        def _():
            skips[0].wait()
            grad[...] += x_skip[...].astype(F32)

        branch[...] = to_low(grad[...])
        keep(branch, o_branch, 0)
        kept[0].wait()
        for start in range(0, hidden_size, BLOCK):
            cut = slice(start, start + BLOCK)
            hidden_low = to_low(matmul(branch[...], w_down[:, cut]) * slope[:, cut].astype(F32))
            hid[:, cut] = hidden_low
            part = matmul(hidden_low, w_up[cut, :])
            if start == 0:
                acc[...] = part
            else:
                acc[...] += part
        keep(hid, o_hid, 1)
        kept[1].wait()
        back, gain_back = normalize_back(acc[...], mid[...], gains[1:2, :])
        gain_g[1:2, :] = gain_back
        grad[...] += back
        proj[...] = to_low(grad[...])
        keep(proj, o_proj, 2)
        for start in range(0, width, BLOCK):
            cut = slice(start, start + BLOCK)
            ctx_g[:, cut] = to_low(matmul(proj[...], w_attn[3 * width :, cut]))
        kept[2].wait()
        kept[3].wait()
        low_half = head_masks(rows)
        for two in range(HEADS // 2):
            cut = slice(two * 128, two * 128 + 128)
            key_cut = slice(width + two * 128, width + two * 128 + 128)
            value_cut = slice(2 * width + two * 128, 2 * width + two * 128 + 128)
            outer_grad = split_heads(ctx_g[:, cut], low_half)
            prob_grad = matmul_nt(outer_grad, qkv[:, value_cut])
            chances = jnp.concatenate([prob[2 * two], prob[2 * two + 1]], axis=0)
            qkvg[:, value_cut] = to_low(matmul_tn(to_low(chances), outer_grad))
            total = jnp.sum(prob_grad * chances, axis=-1, keepdims=True)
            score_grad = to_low(chances * (prob_grad - total))
            query_grad = matmul(score_grad, qkv[:, key_cut]) * 0.125
            qkvg[:, cut] = to_low(jnp.where(low_half, query_grad[:rows], query_grad[rows:]))
            queries = split_heads(qkv[:, cut], low_half)
            qkvg[:, key_cut] = to_low(matmul_tn(score_grad, queries) * 0.125)
        keep(qkvg, o_qkvg, 3)
        for start in range(0, 3 * width, BLOCK):
            cut = slice(start, start + BLOCK)
            part = matmul(qkvg[:, cut], w_attn[cut, :])
            if start == 0:
                acc[...] = part
            else:
                acc[...] += part
        kept[4].wait()
        back, gain_back = normalize_back(acc[...], res[...], gains[0:1, :])
        gain_g[0:1, :] = gain_back
        gain_g[2:8, :] = jnp.zeros((6, width), F32)
        keep(gain_g, o_gain, 5)
        grad[...] += back
        resg[...] = to_low(grad[...])
        keep(resg, o_resg, 4)

        @pl.when(is_dec == 1)
        def _():
            for start in range(0, width, BLOCK):
                cut = slice(start, start + BLOCK)
                skip_cut = slice(width + start, width + start + BLOCK)
                input_grad = to_low(matmul(resg[...], w_skip[:, cut]))
                skip_grad = matmul(resg[...], w_skip[:, skip_cut])
                both = to_low(input_grad.astype(F32) + skip_grad)
                joined[:, cut] = jnp.where(pair == 3, both, input_grad)
                joined[:, skip_cut] = to_low(skip_grad)
            first = pltpu.make_async_copy(joined.at[:, pl.ds(0, width)], leaving, sem_in.at[0])
            second = pltpu.make_async_copy(
                joined.at[:, pl.ds(width, width)], leaving_skip, sem_in.at[1]
            )
            first.start()
            second.start()
            first.wait()
            second.wait()

        @pl.when(is_dec == 0)
        def _():
            first = pltpu.make_async_copy(resg, leaving, sem_in.at[0])
            first.start()
            first.wait()

        for copy in outgoing:
            copy.wait()


def kept_shapes(slots, rows, width, hidden_size):
    return [
        ((slots, rows, 2 * width), BF16),
        ((slots, rows, width), F32),
        ((slots, rows, width), BF16),
        ((slots, rows, 3 * width), BF16),
        ((slots, HEADS, rows, rows), F32),
        ((slots, rows, width), BF16),
        ((slots, rows, width), F32),
        ((slots, rows, width), BF16),
        ((slots, rows, hidden_size), BF16),
        ((slots, rows, hidden_size), BF16),
        ((slots, rows, width), BF16),
    ]


def grad_shapes(slots, rows, width, hidden_size):
    return [
        ((slots, rows, width), BF16),
        ((slots, rows, hidden_size), BF16),
        ((slots, rows, width), BF16),
        ((slots, rows, 3 * width), BF16),
        ((slots, rows, width), BF16),
        ((slots, 8, width), F32),
    ]


ANYWHERE = pl.BlockSpec(memory_space=pl.ANY)
IN_HBM = pl.BlockSpec(memory_space=pltpu.HBM)
IN_VMEM = pl.BlockSpec(memory_space=pltpu.VMEM)
IN_SMEM = pl.BlockSpec(memory_space=pltpu.SMEM)


def stay_in_hbm(array):
    return pltpu.with_memory_space_constraint(array, pltpu.HBM)


def all_ordered(arrays, earlier):
    count = len(arrays)
    return list(
        pl.pallas_call(
            lambda *refs: None,
            out_shape=[pltpu.HBM(array.shape, array.dtype) for array in arrays],
            in_specs=[IN_HBM] * (count + 1),
            out_specs=[IN_HBM] * count,
            input_output_aliases={index: index for index in range(count)},
            compiler_params=pltpu.CompilerParams(vmem_limit_bytes=2**20),
            cost_estimate=QUICK,
            name="ordered",
        )(*arrays, earlier)
    )


def ordered(array, earlier):
    return all_ordered([array], earlier)[0]


def same_in_vmem(arrays):
    return [pltpu.VMEM(array.shape, array.dtype) for array in arrays]


def unwritten(shapes):
    return list(
        pl.pallas_call(
            lambda *refs: None,
            out_shape=[pltpu.HBM(shape, dtype) for shape, dtype in shapes],
            out_specs=[IN_HBM] * len(shapes),
            compiler_params=pltpu.CompilerParams(vmem_limit_bytes=2**20),
            cost_estimate=QUICK,
            name="unwritten",
        )()
    )


def one_slot(shapes):
    return [pltpu.VMEM(shape[1:], dtype) for shape, dtype in shapes]


def forward_tick(base, tick, arrived, embedded, skips, allowed, in_flight, gains, weights, kept):
    slots, rows, width = embedded.shape
    hidden_size = weights[2].shape[1]
    shapes = kept_shapes(slots, rows, width, hidden_size)
    outputs = pl.pallas_call(
        forward_kernel,
        out_shape=[jax.ShapeDtypeStruct((rows, width), BF16)]
        + [pltpu.HBM(shape, dtype) for shape, dtype in shapes]
        + same_in_vmem(weights),
        in_specs=[IN_SMEM] * 2 + [ANYWHERE] * 7 + [IN_VMEM] * 5 + [IN_HBM] * 11,
        out_specs=[ANYWHERE] + [IN_HBM] * 11 + [IN_VMEM] * 4,
        input_output_aliases={14 + index: 1 + index for index in range(11)}
        | {10 + index: 12 + index for index in range(4)},
        scratch_shapes=one_slot(shapes[:1])
        + [pltpu.VMEM((rows, rows), F32)]
        + one_slot(shapes[1:])
        + [
            pltpu.VMEM((rows, width), F32),
            pltpu.SemaphoreType.DMA((3,)),
            pltpu.SemaphoreType.DMA((10,)),
        ],
        compiler_params=pltpu.CompilerParams(vmem_limit_bytes=VMEM_LIMIT),
        cost_estimate=QUICK,
        name="layer_forward",
    )(
        base,
        jnp.array([tick], jnp.int32),
        arrived,
        embedded,
        *skips,
        allowed,
        in_flight,
        gains,
        *weights,
        *kept,
    )
    return outputs[0], list(outputs[1:12]), list(outputs[12:])


def backward_tick(
    base, tick, arrived, head_grads, skips, in_flight, gains, weights, kept, grads
):
    slots, rows, width = head_grads.shape
    hidden_size = weights[2].shape[0]
    shapes = grad_shapes(slots, rows, width, hidden_size)
    was_kept = kept_shapes(slots, rows, width, hidden_size)
    read = [1, 3, 4, 6, 9]
    outputs = pl.pallas_call(
        backward_kernel,
        out_shape=[jax.ShapeDtypeStruct((rows, width), BF16)] * 2
        + [pltpu.HBM(shape, dtype) for shape, dtype in shapes]
        + same_in_vmem(weights),
        in_specs=[IN_SMEM] * 2 + [ANYWHERE] * 6 + [IN_VMEM] * 5 + [IN_HBM] * 11,
        out_specs=[ANYWHERE] * 2 + [IN_HBM] * 6 + [IN_VMEM] * 4,
        input_output_aliases={18 + index: 2 + index for index in range(6)}
        | {9 + index: 8 + index for index in range(4)},
        scratch_shapes=[
            pltpu.VMEM((rows, width), BF16),
            pltpu.VMEM((rows, width), F32),
            pltpu.VMEM((rows, width), BF16),
        ]
        + one_slot([was_kept[index] for index in read])
        + [pltpu.VMEM((rows, width), F32)]
        + one_slot(shapes)
        + [
            pltpu.VMEM((rows, width), F32),
            pltpu.VMEM((rows, width), BF16),
            pltpu.VMEM((rows, 2 * width), BF16),
            pltpu.SemaphoreType.DMA((8,)),
            pltpu.SemaphoreType.DMA((6,)),
        ],
        compiler_params=pltpu.CompilerParams(vmem_limit_bytes=VMEM_LIMIT),
        cost_estimate=QUICK,
        name="layer_backward",
    )(
        base,
        jnp.array([tick], jnp.int32),
        arrived,
        head_grads,
        *skips,
        in_flight,
        gains,
        *weights,
        *[stay_in_hbm(kept[index]) for index in read],
        *grads,
    )
    return outputs[0], outputs[1], list(outputs[2:8]), list(outputs[8:])


def transposed_shapes(weights):
    return [(weight.shape[::-1], BF16) for weight in weights]


def transpose_half(base, weight, target, half, for_dec):
    block = min(512, *weight.shape)

    def kernel(base_ref, source, start, same, out, stage, sems):
        @pl.when((base_ref[0] == (1 if for_dec else 0)) & (base_ref[7] == 0))
        def _():
            waiting = [None, None]
            steps = [
                (row, column)
                for row in range(0, source.shape[0], block)
                for column in range(0, source.shape[1], block)
            ]
            middle = len(steps) // 2
            steps = steps[middle:] if half else steps[:middle]
            for index, (row, column) in enumerate(steps):
                slot = index % 2
                if waiting[slot] is not None:
                    waiting[slot].wait()
                stage[slot] = source[row : row + block, column : column + block].T
                target = out.at[pl.ds(column, block), pl.ds(row, block)]
                waiting[slot] = pltpu.make_async_copy(stage.at[slot], target, sems.at[slot])
                waiting[slot].start()
            for copy in waiting:
                copy.wait()

    return pl.pallas_call(
        kernel,
        out_shape=[*same_in_vmem([weight]), pltpu.HBM(target.shape, target.dtype)],
        in_specs=[IN_SMEM, IN_VMEM, IN_HBM],
        out_specs=[IN_VMEM, IN_HBM],
        input_output_aliases={1: 0, 2: 1},
        scratch_shapes=[pltpu.VMEM((2, block, block), BF16), pltpu.SemaphoreType.DMA((2,))],
        compiler_params=pltpu.CompilerParams(vmem_limit_bytes=VMEM_LIMIT),
        cost_estimate=QUICK,
        name="transpose_half",
    )(base, weight, target)


def head_pass(
    base, final, target, frame_weight, head_rows, out_gain, scale, mel_bins, transposed
):
    slots, rows, width = final.shape
    count_weights = len(transposed)
    def kernel(
        base_ref, scale_ref, final_ref, target_ref, weight_ref, head_ref, gain_ref, *refs
    ):
        sources = refs[:count_weights]
        grads_ref, table_ref, gain_grad_ref, loss_ref = refs[count_weights : count_weights + 4]
        wholes = refs[count_weights + 4 : 2 * count_weights + 4]
        x_buf, out_buf, s_in, s_out, s_weights = refs[2 * count_weights + 4 :]
        moves = [
            pltpu.make_async_copy(source, whole, s_weights.at[index])
            for index, (source, whole) in enumerate(zip(sources, wholes))
        ]

        @pl.when(base_ref[7] == 0)
        def _():
            for move in moves:
                move.start()

        table_ref[...] = jnp.zeros((mel_bins, width), F32)
        gain_grad_ref[...] = jnp.zeros((1, width), F32)
        loss_ref[...] = jnp.zeros((rows, 128), F32)
        is_last = base_ref[2] == base_ref[6]
        count = base_ref[4]

        def row(i):
            load = pltpu.make_async_copy(final_ref.at[i], x_buf.at[i], s_in.at[i])
            load.wait()
            wide = x_buf[i].astype(F32)
            normed = to_low(normalize(wide, gain_ref[...]))
            error = matmul_nt(normed, head_ref[...]) - target_ref[i]
            weight = weight_ref[i]
            loss_ref[...] += weight * (error * error) * (1.0 / mel_bins)
            d_pred = to_low(error * weight * scale_ref[0])
            table_ref[...] += matmul_tn(d_pred, normed)[:mel_bins]
            back, gain_back = normalize_back(matmul(d_pred, head_ref[...]), wide, gain_ref[...])
            gain_grad_ref[...] += gain_back
            out_buf[i] = back
            pltpu.make_async_copy(out_buf.at[i], grads_ref.at[i], s_out.at[i]).start()

        @pl.when(is_last)
        def _():
            for i in range(slots):

                @pl.when(i < count)
                def _():
                    pltpu.make_async_copy(final_ref.at[i], x_buf.at[i], s_in.at[i]).start()

            for i in range(slots):
                pl.when(i < count)(lambda i=i: row(i))
            for i in range(slots):

                @pl.when(i < count)
                def _():
                    pltpu.make_async_copy(out_buf.at[i], grads_ref.at[i], s_out.at[i]).wait()

        @pl.when(base_ref[7] == 0)
        def _():
            for move in moves:
                move.wait()

    return pl.pallas_call(
        kernel,
        out_shape=[
            pltpu.HBM((slots, rows, width), F32),
            jax.ShapeDtypeStruct((mel_bins, width), F32),
            jax.ShapeDtypeStruct((1, width), F32),
            jax.ShapeDtypeStruct((rows, 128), F32),
        ]
        + same_in_vmem(transposed),
        in_specs=[IN_SMEM] * 2 + [IN_HBM] + [IN_VMEM] * 4 + [IN_HBM] * count_weights,
        out_specs=[IN_HBM] + [IN_VMEM] * (3 + count_weights),
        scratch_shapes=[
            pltpu.VMEM((slots, rows, width), BF16),
            pltpu.VMEM((slots, rows, width), F32),
            pltpu.SemaphoreType.DMA((slots,)),
            pltpu.SemaphoreType.DMA((slots,)),
            pltpu.SemaphoreType.DMA((count_weights,)),
        ],
        compiler_params=pltpu.CompilerParams(vmem_limit_bytes=VMEM_LIMIT),
        cost_estimate=QUICK,
        name="head_pass",
    )(base, scale, final, target, frame_weight, head_rows, out_gain, *transposed)


def table_pass(
    base, front, input_grads, gain_grads, head_total, out_gain_total, table_rows, earlier
):
    slots, rows, width = input_grads.shape
    front_rows, mel_bins = front.shape[1], head_total.shape[0]

    def kernel(
        base_ref, front_ref, grad_ref, gain_ref, earlier_ref, head_ref, out_ref, block_ref, x, y, g, sems
    ):
        is_dec = base_ref[0] == 1
        is_outer = base_ref[7] == 1
        block_ref[...] = jnp.zeros((table_rows + 16, width), BF16)
        tail = table_rows - front_rows - mel_bins
        block_ref[front_rows : front_rows + mel_bins, :] = to_low(head_ref[...])
        first = lax.broadcasted_iota(jnp.int32, (tail, width), 0) == 0
        block_ref[front_rows + mel_bins : table_rows, :] = to_low(
            jnp.where(first, out_ref[...], 0.0)
        )

        @pl.when(jnp.logical_not(is_outer))
        def _():
            load = pltpu.make_async_copy(gain_ref, g, sems.at[2])
            load.start()
            load.wait()
            total = g[0]
            for i in range(1, slots):
                total = total + g[i]
            own = jnp.concatenate([total, jnp.zeros((8, width), F32)], axis=0)
            moved = jnp.concatenate([jnp.zeros((2, width), F32), own[:14]], axis=0)
            block_ref[table_rows:, :] = to_low(jnp.where(is_dec, moved, own))

        @pl.when((base_ref[2] == 0) & jnp.logical_not(is_outer))
        def _():
            loads = [
                pltpu.make_async_copy(front_ref, x, sems.at[0]),
                pltpu.make_async_copy(grad_ref, y, sems.at[1]),
            ]
            for load in loads:
                load.start()
            for load in loads:
                load.wait()
            product = matmul_tn(x[...], y[...].reshape(slots * rows, width))
            block_ref[:front_rows, :] = to_low(product)

    return pl.pallas_call(
        kernel,
        out_shape=jax.ShapeDtypeStruct((table_rows + 16, width), BF16),
        in_specs=[IN_SMEM] + [IN_HBM] * 4 + [IN_VMEM] * 2,
        out_specs=IN_VMEM,
        scratch_shapes=[
            pltpu.VMEM(front.shape, BF16),
            pltpu.VMEM(input_grads.shape, BF16),
            pltpu.VMEM(gain_grads.shape, F32),
            pltpu.SemaphoreType.DMA((3,)),
        ],
        compiler_params=pltpu.CompilerParams(vmem_limit_bytes=VMEM_LIMIT),
        cost_estimate=QUICK,
        name="table_pass",
    )(
        base, stay_in_hbm(front), input_grads, gain_grads, stay_in_hbm(earlier), head_total,
        out_gain_total,
    )


def assemble(base, main_shards, skip_shards, span, width, hidden_size):
    main = [part for group in main_shards for part in group]
    skip = [part for group in skip_shards for part in group]
    sides = hidden_size // width
    per_main = 2 + sides

    def kernel(base_ref, *refs):
        main_refs, skip_refs = refs[: len(main)], refs[len(main) : len(main) + len(skip)]
        w_skip, w_attn, w_up, w_down, s_main, s_skip = refs[len(main) + len(skip) :]
        is_dec, quarter, rank = base_ref[0] == 1, base_ref[8], base_ref[9]
        which = [quarter, quarter ^ 1, jnp.where(is_dec, 1, 2), jnp.where(is_dec, 0, 3)]

        def rows_of(index, count):
            shard = which[index % 4] * span + (rank ^ (index // 4))
            return pl.multiple_of(shard * count, count)

        @pl.when(base_ref[7] == 0)
        def _():
            copies, skip_copies = [], []
            for index, source in enumerate(skip_refs):
                count = source.shape[0]
                target = w_skip.at[pl.ds(rows_of(index, count), count)]
                skip_copies.append(pltpu.make_async_copy(source, target, s_skip.at[index]))
            for index, source in enumerate(main_refs):
                count = source.shape[1]
                start = rows_of(index, count)
                sems = s_main.at[index]
                for place, whole in enumerate((w_attn, w_up)):
                    target = whole.at[pl.ds(start, count)]
                    copies.append(pltpu.make_async_copy(source.at[place], target, sems.at[place]))
                for side in range(sides):
                    block = source.at[2, :, pl.ds(side * width, width)]
                    row = pl.multiple_of(start * sides + side * count, count)
                    target = w_down.at[pl.ds(row, count)]
                    copies.append(pltpu.make_async_copy(block, target, sems.at[2 + side]))

            @pl.when(is_dec)
            def _():
                for copy in skip_copies:
                    copy.start()

            for copy in copies:
                copy.start()
            for copy in copies:
                copy.wait()

            @pl.when(is_dec)
            def _():
                for copy in skip_copies:
                    copy.wait()

    return list(
        pl.pallas_call(
            kernel,
            out_shape=[
                pltpu.VMEM((2 * width, width), BF16),
                pltpu.VMEM((width, 4 * width), BF16),
                pltpu.VMEM((width, hidden_size), BF16),
                pltpu.VMEM((hidden_size, width), BF16),
            ],
            in_specs=[IN_SMEM] + [IN_HBM] * (len(main) + len(skip)),
            out_specs=[IN_VMEM] * 4,
            scratch_shapes=[
                pltpu.SemaphoreType.DMA((len(main), per_main)),
                pltpu.SemaphoreType.DMA((len(skip),)),
            ],
            compiler_params=pltpu.CompilerParams(vmem_limit_bytes=VMEM_LIMIT),
            cost_estimate=QUICK,
            name="assemble",
        )(base, *(stay_in_hbm(part) for part in main + skip))
    )


def weight_products(base, first, slots_used, span, specs, lefts, rights, came, earlier):
    names_left, names_right = list(lefts), list(rights)
    direct = {name: lefts[name].ndim == 3 for name in names_left}
    units = []
    for matrix, (rows, cols, blocks) in enumerate(specs):
        quads = [tuple(range(4))] if 4 * rows <= 512 else [(q,) for q in range(4)]
        for left, right, source, column, size in blocks:
            for quad in quads:
                units.append((matrix, quad, rows, left, right, source, column, size))
    steps = [(other, unit) for other in (range(1, span) if first else (0,)) for unit in units]
    left_width = max(-(-len(quad) * rows // 128) * 128 for _, quad, rows, *_ in units)
    right_width = max(unit[7] for unit in units)
    side_cols = max(cols for _, cols, _ in specs)
    side_rows = min(rows for rows, _, _ in specs)
    outs = []
    if first:
        for rows, cols, _ in specs:
            outs += [pltpu.HBM((4, rows, cols), BF16)] * (span - 1)
    else:
        outs += [pltpu.HBM((len(specs), side_rows, side_cols), BF16)] * 3
        outs += [pltpu.HBM((rows, cols), F32) for rows, cols, _ in specs]
        outs += [pltpu.HBM((8, right_width), F32)]
    n_in = len(names_left) + len(names_right)
    n_came = len(came)

    def kernel(base_ref, *refs):
        left_refs = dict(zip(names_left, refs))
        right_refs = dict(zip(names_right, refs[len(names_left) :]))
        came_refs = refs[n_in : n_in + n_came]
        at = n_in + n_came + len(earlier)
        out_refs = refs[at : at + len(outs)]
        x_buf, y_buf, came_buf, low_buf, own_buf, sum_buf, s_x, s_y, s_came, s_out = refs[
            at + len(outs) :
        ]
        is_dec, rank = base_ref[0], base_ref[9]
        edge = jnp.where(is_dec == 1, 3, 0)
        own = jnp.where(is_dec == 1, 2, 1)
        near, far = jnp.where(is_dec == 1, 1, 2), jnp.where(is_dec == 1, 0, 3)

        def loads(index):
            other, (matrix, quad, rows, left, right, source, column, size) = steps[index]
            slot = index % 2
            copies = []
            for place, q in enumerate(quad):
                if direct[left]:
                    start = pl.multiple_of((q * span + (rank ^ other)) * rows, 128)
                    block = left_refs[left].at[pl.ds(0, slots_used), :, pl.ds(start, rows)]
                    target = x_buf.at[slot, :, :, pl.ds(place * rows, rows)]
                elif place == 0:
                    block = left_refs[left].at[rank ^ other, pl.ds(0, slots_used)]
                    target = x_buf.at[slot, :, :, pl.ds(0, lefts[left].shape[3])]
                else:
                    continue
                copies.append((block, target, s_x.at[slot, place]))
            block = right_refs[right].at[pl.ds(0, slots_used), :, pl.ds(source, size)]
            copies.append((block, y_buf.at[slot, :, :, pl.ds(0, size)], s_y.at[slot]))
            return [pltpu.make_async_copy(*copy) for copy in copies]

        def add_loads(index):
            _, (matrix, quad, rows, left, right, source, column, size) = steps[index]
            count = len(quad)
            copies = []
            for other in range(n_came // len(specs)):
                block = came_refs[matrix * (span - 1) + other].at[
                    pl.ds(quad[0], count), :, pl.ds(column, size)
                ]
                target = came_buf.at[other, pl.ds(0, count), pl.ds(0, rows), pl.ds(0, size)]
                copies.append(pltpu.make_async_copy(block, target, s_came.at[other]))
            return copies

        def run():
            for copy in loads(0):
                copy.start()
            sum_buf[...] = jnp.zeros(sum_buf.shape, F32)
            pending = {0: [], 1: []}
            for index, (other, unit) in enumerate(steps):
                matrix, quad, rows, left, right, source, column, size = unit
                slot, count = index % 2, len(quad)
                if index + 1 < len(steps):
                    for copy in loads(index + 1):
                        copy.start()
                adds = [] if first else add_loads(index)
                for copy in adds:
                    copy.start()
                for copy in loads(index):
                    copy.wait()
                deep = slots_used * x_buf.shape[2]
                x = x_buf[slot, :, :, : count * rows].reshape(deep, count * rows)
                y = y_buf[slot, :, :, :size].reshape(deep, size)
                total = matmul_tn(x, y).reshape(count, rows, size)
                for copy in adds:
                    copy.wait()
                for which in range(len(adds)):
                    total = total + came_buf[which, :count, :rows, :size].astype(F32)
                for copy in pending[slot]:
                    copy()
                pending[slot] = []
                low_buf[slot, :count, :rows, :size] = to_low(total)

                def send(block, target, sem, condition=None):
                    copy = pltpu.make_async_copy(block, target, sem)
                    if condition is None:
                        copy.start()
                        pending[slot].append(copy.wait)
                        return

                    @pl.when(condition)
                    def _():
                        copy.start()

                    def wait():
                        @pl.when(condition)
                        def _():
                            copy.wait()

                    pending[slot].append(wait)

                staged = low_buf.at[slot, :, pl.ds(0, rows), pl.ds(0, size)]
                wide = own_buf.at[slot, pl.ds(0, rows), pl.ds(0, size)]
                cut = pl.ds(column, size)
                if first:
                    send(
                        staged.at[pl.ds(0, count)],
                        out_refs[matrix * (span - 1) + other - 1].at[pl.ds(quad[0], count), :, cut],
                        s_out.at[slot, 0, 0],
                    )
                    continue
                parts = rows // side_rows
                for place, whose in enumerate((edge, near, far)):
                    for part in range(parts):
                        target = out_refs[place].at[
                            matrix, :, pl.ds(part * side_cols // parts + column, size)
                        ]
                        source = staged.at[
                            whose if count == 4 else 0, pl.ds(part * side_rows, side_rows)
                        ]
                        condition = None if count == 4 else whose == quad[0]
                        send(source, target, s_out.at[slot, place, part], condition)
                for place, q in enumerate(quad):

                    @pl.when(own == q)
                    def _():
                        own_buf[slot, :rows, :size] = total[place]
                        squares = (total[place] * total[place]).reshape(-1, 8, size)
                        sum_buf[:, :size] += jnp.sum(squares, axis=0)

                condition = None if count == 4 else own == quad[0]
                send(wide, out_refs[3 + matrix].at[:, cut], s_out.at[slot, 3, 0], condition)
            for slot in (0, 1):
                for copy in pending[slot]:
                    copy()
            if not first:
                copy = pltpu.make_async_copy(sum_buf, out_refs[-1], s_y.at[0])
                copy.start()
                copy.wait()

        pl.when(base_ref[7] == 0)(run)

    row_len = rights[names_right[0]].shape[1]
    tall = max(rows for rows, _, _ in specs)
    quad_rows = max(len(quad) for _, quad, *_ in units)
    results = pl.pallas_call(
        kernel,
        out_shape=outs,
        in_specs=[IN_SMEM] + [IN_HBM] * (n_in + n_came + len(earlier)),
        out_specs=[IN_HBM] * len(outs),
        scratch_shapes=[
            pltpu.VMEM((2, slots_used, row_len, left_width), BF16),
            pltpu.VMEM((2, slots_used, row_len, right_width), BF16),
            pltpu.VMEM((max(n_came // len(specs), 1), quad_rows, tall, right_width), BF16),
            pltpu.VMEM((2, quad_rows, tall, right_width), BF16),
            pltpu.VMEM((2, tall, right_width), F32),
            pltpu.VMEM((8, right_width), F32),
            pltpu.SemaphoreType.DMA((2, 4)),
            pltpu.SemaphoreType.DMA((2,)),
            pltpu.SemaphoreType.DMA((max(span - 1, 1),)),
            pltpu.SemaphoreType.DMA((2, 4, tall // side_rows)),
        ],
        compiler_params=pltpu.CompilerParams(vmem_limit_bytes=2 * VMEM_LIMIT),
        cost_estimate=QUICK,
        name="weight_products",
    )(base, *(stay_in_hbm(a) for a in (*lefts.values(), *rights.values(), *came, *earlier)))
    return list(results)


def adam_update(master, first, second, gradient, factor, step_rate):
    gradient = gradient * factor
    first_new = beta_one * first + (1.0 - beta_one) * gradient
    second_new = beta_two * second + (1.0 - beta_two) * gradient * gradient
    corrected = first_new / (1.0 - beta_one**STEP)
    spread = jnp.sqrt(second_new / (1.0 - beta_two**STEP))
    master_new = master - step_rate * (corrected / (spread + adam_eps) + weight_decay * master)
    return (master_new, first_new, second_new, master_new.astype(BF16))


def body(
    clean_mel,
    noise,
    phone_ids,
    segment_ids,
    loss_mask,
    time_idx,
    attn_w,
    attn_m,
    attn_v,
    up_w,
    up_m,
    up_v,
    down_w,
    down_m,
    down_v,
    skip_w,
    skip_m,
    skip_v,
    gain_w,
    gain_m,
    gain_v,
    table_w,
    table_m,
    table_v,
):
    sections = lax.axis_size("section")
    batch = lax.axis_size("batch")
    section_id = lax.axis_index("section")
    batch_id = lax.axis_index("batch")
    span = batch // 4
    quarter, rank = batch_id // span, batch_id % span
    is_dec = quarter >= 2
    is_outer = (quarter == 0) | (quarter == 3)
    local_rows, row_len, mel_bins = clean_mel.shape
    width = attn_w.shape[3] // 4
    hidden_size = up_w.shape[3]
    total_rows = local_rows * batch
    slots = total_rows // span
    top = 2 * sections - 1
    pos = jnp.where(is_dec, top - section_id, section_id)
    chain_rows = jnp.where(is_outer, 0, slots)
    base = jnp.stack(
        [is_dec, section_id, pos, 0, chain_rows, slots, top, is_outer, quarter, rank]
    ).astype(jnp.int32)

    near, far, back_far = ((1, 2), (2, 1)), ((0, 2), (3, 1)), ((1, 3), (2, 0))
    inward, outward = ((0, 1), (3, 2)), ((1, 0), (2, 3))

    def along(block, pairs):
        route = [(a * span + i, b * span + i) for a, b in pairs for i in range(span)]
        return lax.ppermute(block, "batch", route)

    def across(block, bits, members=(0, 1, 2, 3)):
        route = [(a * span + i, a * span + (i ^ bits)) for a in members for i in range(span)]
        return lax.ppermute(block, "batch", route)

    def flipped(block, axis, bit):
        return lax.ppermute(block, axis, [(i, i ^ bit) for i in range(lax.axis_size(axis))])

    def at_stage(stage):
        return (stage, 1) if stage < sections else (top - stage, 2)

    def stage_route(pairs):
        route = []
        for source, target in pairs:
            (s, a), (t, b) = at_stage(source), at_stage(target)
            route += [(s * batch + a * span + i, t * batch + b * span + i) for i in range(span)]
        return route

    chain_forward = stage_route([(stage, stage + 1) for stage in range(top)])
    chain_backward = stage_route([(stage + 1, stage) for stage in range(top)])
    skip_forward = stage_route([(s, top - s) for s in range(sections - 1)])
    skip_backward = stage_route([(top - s, s) for s in range(sections - 1)])

    times = jnp.stack([time_idx // 32, time_idx % 32], axis=1)
    small = [
        clean_mel.reshape(-1),
        noise.reshape(-1),
        to_low(jnp.stack([phone_ids, segment_ids, loss_mask], axis=1)).reshape(-1),
        to_low(times).reshape(-1),
        to_low(gain_w[0]).reshape(-1),
    ]
    sizes = [part.size for part in small]
    packed = jnp.pad(jnp.concatenate(small), (0, -sum(sizes) % 1024)).reshape(1, -1, 128)
    everyone = lax.all_gather(packed, "batch", axis=0, tiled=True).reshape(batch, -1)
    parts = []
    offset = 0
    for size in sizes:
        parts.append(everyone[:, offset : offset + size])
        offset += size

    def every_rank(piece, members):
        return [piece] + [across(piece, bits, members) for bits in range(1, span)]

    def gather_shards(enc_part, dec_part, only_dec):
        limit = (lambda pairs: tuple(p for p in pairs if p[1] >= 2)) if only_dec else (lambda p: p)
        members = (2,) if only_dec else (1, 2)
        own = ordered(jnp.where(is_dec, dec_part, enc_part), everyone)
        other = ordered(jnp.where(is_dec, enc_part, dec_part), everyone)
        pieces = (
            own,
            along(own, limit(inward)),
            along(other, limit(near)),
            along(other, limit(far)),
        )
        return [list(group) for group in zip(*(every_rank(p, members) for p in pieces))]

    def packed_shard(layer):
        rows = width // batch
        down = to_low(down_w[0, layer])
        side = [down[i * rows : (i + 1) * rows] for i in range(hidden_size // width)]
        return jnp.stack(
            [to_low(attn_w[0, layer]), to_low(up_w[0, layer]), jnp.concatenate(side, axis=1)]
        )

    skip_low = to_low(skip_w[0])
    skip_shards = gather_shards(skip_low, skip_low, True)
    main_shards = gather_shards(packed_shard(0), packed_shard(1), False)
    weights = assemble(base, main_shards, skip_shards, span, width, hidden_size)

    all_clean = parts[0].reshape(total_rows, row_len, mel_bins)
    all_noise = parts[1].reshape(total_rows, row_len, mel_bins)
    all_ids = parts[2].reshape(total_rows, 3, row_len).astype(F32)
    all_times = parts[3].reshape(total_rows, 2).astype(F32)
    all_gains = parts[4].reshape(batch, 4, width // batch)
    all_gains = jnp.moveaxis(all_gains, 0, 1).reshape(4, width).astype(F32)
    gains = jnp.where(is_dec, all_gains[2:4], all_gains[0:2])
    mask_total = jnp.sum(all_ids[:, 2])

    def chain_part(array):
        return lax.dynamic_slice_in_dim(array, rank * slots, slots, 0)

    clean_rows = chain_part(all_clean).astype(F32)
    noise_rows = chain_part(all_noise).astype(F32)
    ids = chain_part(all_ids)
    time_parts = chain_part(all_times)
    phones, segments, weight = ids[:, 0], ids[:, 1], ids[:, 2]
    flow_time = (time_parts[:, 0] * 32.0 + time_parts[:, 1]) / TSTEPS
    wide_time = flow_time[:, None, None]
    noisy_mel = (1.0 - (1.0 - sigma_min) * wide_time) * noise_rows + wide_time * clean_rows
    context_mel = clean_rows * (1.0 - weight)[..., None]
    target = clean_rows - (1.0 - sigma_min) * noise_rows
    onehot = to_low(phones[..., None] == jnp.arange(VOCAB, dtype=F32))
    front = jnp.concatenate([to_low(noisy_mel), to_low(context_mel), onehot], axis=2)
    half = width // 2
    frequency = jnp.exp(-math.log(10000.0) * jnp.arange(half, dtype=F32) / half) * (
        1000.0 * flow_time[:, None]
    )
    timing = jnp.concatenate([jnp.sin(frequency), jnp.cos(frequency)], axis=1)
    table_low = to_low(table_w)
    front_rows = 2 * mel_bins + VOCAB
    head_rows = table_low[front_rows : front_rows + mel_bins]
    out_gain = table_low[front_rows + mel_bins].astype(F32)[None]
    flat_front = front.reshape(slots * row_len, front_rows)
    embedded = (
        matmul(flat_front[:, : 2 * mel_bins], table_low[: 2 * mel_bins])
        + matmul(flat_front[:, 2 * mel_bins :], table_low[2 * mel_bins : front_rows])
    ).reshape(slots, row_len, width)
    embedded = to_low(embedded + timing[:, None, :])
    allowed = (segments[:, :, None] == segments[:, None, :]).astype(F32)
    frame_weight = jnp.broadcast_to(weight[..., None], (slots, row_len, 128))
    target = jnp.pad(target, ((0, 0), (0, 0), (0, 128 - mel_bins)))
    head_rows = jnp.pad(head_rows, ((0, 128 - mel_bins), (0, 0)))
    scale = (2.0 / (mel_bins * mask_total))[None]
    base, embedded, allowed, frame_weight, target, head_rows, out_gain, scale, flat_front = (
        lax.optimization_barrier(
            (base, embedded, allowed, frame_weight, target, head_rows, out_gain, scale, flat_front)
        )
    )
    embedded, allowed = stay_in_hbm(embedded), stay_in_hbm(allowed)

    kept = unwritten(kept_shapes(slots, row_len, width, hidden_size))
    transposed = unwritten(transposed_shapes(weights))
    blank = jnp.zeros((row_len, width), BF16)
    waits = [LAG * (top - 2 * s) for s in range(sections - 1)]
    soon = 2 * LAG
    tick_count = LAG * top + slots
    skip_sent, arriving = [], []
    for tick in range(tick_count):
        arrived = arriving[tick - LAG] if tick >= LAG else blank
        skips = [skip_sent[tick - wait] if tick >= wait else blank for wait in waits]
        in_flight = skip_sent[tick - soon] if tick >= soon else blank
        for for_dec, begin in ((True, 0), (False, LAG * (sections - 1) + slots - 2)):
            which, half = (tick - begin) // 2, (tick - begin) % 2
            if tick in range(begin, begin + 2 * len(weights)) and (for_dec or which):
                weights[which], transposed[which] = transpose_half(
                    base, weights[which], transposed[which], half, for_dec
                )
        output, kept, weights = forward_tick(
            base, tick, arrived, embedded, skips, allowed, in_flight, gains, weights, kept
        )
        arriving.append(lax.ppermute(output, BOTH, chain_forward))
        is_needed = tick < LAG * (sections - 2) + slots
        skip_sent.append(lax.ppermute(output, BOTH, skip_forward) if is_needed else blank)

    head_grads, head_total, out_gain_total, loss_parts, *weights = head_pass(
        base, kept[10], target, frame_weight, head_rows, out_gain, scale, mel_bins, transposed
    )

    head_grads = stay_in_hbm(head_grads)

    grads = unwritten(grad_shapes(slots, row_len, width, hidden_size))
    skip_sent, arriving = [], []
    for tick in range(tick_count):
        arrived = arriving[tick - LAG] if tick >= LAG else blank
        skips = [skip_sent[tick - wait] if tick >= wait else blank for wait in waits]
        in_flight = skip_sent[tick - soon] if tick >= soon else blank
        output, skip_output, grads, weights = backward_tick(
            base, tick, arrived, head_grads, skips, in_flight, gains, weights, kept, grads
        )
        arriving.append(lax.ppermute(output, BOTH, chain_backward))
        is_needed = tick < LAG * (sections - 2) + slots
        skip_sent.append(lax.ppermute(skip_output, BOTH, skip_backward) if is_needed else blank)

    columns = min(1024, width)
    attn_blocks = [
        ("ain", "qkvg", start, start, columns) for start in range(0, 3 * width, columns)
    ] + [("ctx", "proj", start, 3 * width + start, columns) for start in range(0, width, columns)]
    specs = {
        "down": (
            hidden_size // batch,
            width,
            [("act", "branch", start, start, columns) for start in range(0, width, columns)],
        ),
        "up": (
            width // batch,
            hidden_size,
            [("fin", "hid", start, start, columns) for start in range(0, hidden_size, columns)],
        ),
        "attn": (width // batch, 4 * width, attn_blocks),
        "skip": (
            2 * width // batch,
            width,
            [("join", "resg", start, start, columns) for start in range(0, width, columns)],
        ),
    }
    lefts = dict(zip(("join", "ain", "ctx", "fin", "act"), (kept[i] for i in (0, 2, 5, 7, 8))))
    rights = dict(zip(("branch", "hid", "proj", "qkvg", "resg"), grads))

    def lefts_of(name):
        rows = specs[name][0]
        found = {}
        for left in dict.fromkeys(block[0] for block in specs[name][2]):
            array = lefts[left]
            if rows % 128:
                array = array.reshape(slots, row_len, 4, span, rows)
                array = jnp.moveaxis(array, 3, 0).reshape(span, slots, row_len, 4 * rows)
                array = jnp.pad(array, ((0, 0),) * 3 + ((0, -4 * rows % 128),))
            found[left] = array
        return found

    def products(names, first, came, earlier):
        wanted = dict.fromkeys(block[1] for name in names for block in specs[name][2])
        found = {}
        for name in names:
            found |= lefts_of(name)
        return weight_products(
            base,
            first,
            slots,
            span,
            [specs[name] for name in names],
            found,
            {right: rights[right] for right in wanted},
            came,
            [stay_in_hbm(array) for array in earlier],
        )

    groups = (("skip",), ("up", "down", "attn"))
    came, own_grads, arrived_grads, own_squares = {}, {}, {}, {}
    earlier = []
    for names in groups:
        sent = products(names, True, [], earlier)
        if not earlier:
            table_earlier = sent[0]
        earlier = sent[:1]
        members = (2,) if names == ("skip",) else (1, 2)
        bits = [1 + i % (span - 1) for i in range(len(sent))]
        came[names] = [across(part, bit, members) for part, bit in zip(sent, bits)]

    for names in groups:
        results = products(names, False, came[names], earlier)
        earlier = results[:1]
        limit = (
            (lambda pairs: tuple(p for p in pairs if p[0] >= 2))
            if names == ("skip",)
            else (lambda pairs: pairs)
        )
        arrived_grads[names] = [
            along(part, limit(pairs)) for part, pairs in zip(results, (outward, near, back_far))
        ]
        own_grads |= dict(zip(names, results[3:-1]))
        own_squares[names] = results[-1]

    table_count = front_rows + mel_bins + 1
    table_rows = -(-table_count // (16 * span)) * 16 * span
    shared = table_pass(
        base, flat_front, grads[4], grads[5], head_total, out_gain_total, table_rows, table_earlier
    )
    bit = 1
    while bit < span:
        shared = shared + across(shared, bit)
        bit *= 2
    share = table_rows // span
    mine = lax.dynamic_slice_in_dim(shared, rank * share, share, 0)
    first_rank = (rank == 0) & ~is_outer
    small_squares = jnp.sum(mine.astype(F32) ** 2) + jnp.where(
        first_rank, jnp.sum(shared[table_rows:].astype(F32) ** 2), 0.0
    )
    mine = jnp.concatenate([mine, shared[table_rows:]])
    mine = mine + along(mine, near)
    mine = mine + along(mine, outward)
    gain_rows = mine[share : share + 4].astype(F32)
    mine = mine[:share]
    bit = 1
    while bit < sections:
        mine = mine + flipped(mine, "section", bit)
        bit *= 2
    table_parts = [mine] + [across(mine, bits) for bits in range(1, span)]
    table_grad = jnp.zeros((table_rows, width), BF16)
    for bits, part in enumerate(table_parts):
        table_grad = lax.dynamic_update_slice_in_dim(table_grad, part, (rank ^ bits) * share, 0)
    gain_grad = lax.dynamic_slice_in_dim(
        gain_rows, batch_id * (width // batch), width // batch, 1
    )


    def squares_of(names):
        edge, close, distant = (part.astype(F32) for part in arrived_grads[names])
        has_own = (quarter == 2) if names == ("skip",) else ~is_outer
        own = jnp.where(has_own, jnp.sum(own_squares[names]), 0.0)
        return own + jnp.sum(edge * edge + close * close + distant * distant)

    squares = sum(squares_of(names) for names in groups) + small_squares
    loss_local = jnp.where(is_outer, 0.0, jnp.sum(loss_parts))
    lane = lax.broadcasted_iota(jnp.int32, (8, 128), 1)
    sums = jnp.where(lane == 0, squares, jnp.where(lane == 1, loss_local, 0.0))
    for axis, size in (("batch", batch), ("section", sections)):
        bit = 1
        while bit < size:
            sums = sums + flipped(sums, axis, bit)
            bit *= 2
    loss_sum = sums[0, 1]
    grad_norm = jnp.sqrt(sums[0, 0])
    factor = clip_norm / jnp.maximum(grad_norm, clip_norm)

    def both_layers(name):
        index = groups[1].index(name)
        edge, close, distant = (part[index] for part in arrived_grads[groups[1]])
        if name == "down":
            edge, close, distant = (
                jnp.concatenate(
                    [part[:, i * width : (i + 1) * width] for i in range(hidden_size // width)]
                )
                for part in (edge, close, distant)
            )
        own = jnp.where(is_outer, edge.astype(F32), own_grads[name])
        other = jnp.where(is_outer, distant, close).astype(F32)
        return jnp.stack([jnp.where(is_dec, other, own), jnp.where(is_dec, own, other)])[None]

    attn_out = adam_update(attn_w, attn_m, attn_v, both_layers("attn"), factor, rate_matrix)
    up_out = adam_update(up_w, up_m, up_v, both_layers("up"), factor, rate_matrix)
    down_out = adam_update(down_w, down_m, down_v, both_layers("down"), factor, rate_matrix)
    edge, close, distant = (part[0].astype(F32) for part in arrived_grads[groups[0]])
    skip_grad = jnp.where(
        is_dec, jnp.where(is_outer, edge, own_grads["skip"]), jnp.where(is_outer, distant, close)
    )
    skip_out = adam_update(skip_w, skip_m, skip_v, skip_grad[None], factor, rate_matrix)
    table_grad = table_grad[:table_count].astype(F32)
    gain_out = adam_update(gain_w, gain_m, gain_v, gain_grad[None], factor, rate_gain)
    table_out = adam_update(table_w, table_m, table_v, table_grad, factor, rate_table)
    return (
        loss_sum, mask_total, grad_norm,
        *attn_out, *up_out, *down_out, *skip_out, *gain_out, *table_out,
    )


def solution(mesh):
    row_specs = (
        P("batch", None, None),
        P("batch", None, None),
        P("batch", None),
        P("batch", None),
        P("batch", None),
        P("batch"),
    )
    wide = P("section", None, "batch", None)
    flat = P("section", "batch", None)
    gain = P("section", None, "batch")
    return jax.shard_map(
        body,
        mesh=mesh,
        in_specs=row_specs + (wide,) * 9 + (flat,) * 3 + (gain,) * 3 + (P(),) * 3,
        out_specs=(P(),) * 3 + (wide,) * 12 + (flat,) * 4 + (gain,) * 4 + (P(),) * 4,
        check_vma=False,
    )
```
